256 devices in a mesh: grp: 8 (over z_lo, core), dev: 32 (over z_hi, x, y).
Axes of the slice: x: 4, y: 4, z: 8 (z_hi: 2, z_lo: 4; z = z_hi * 4 + z_lo), core: 2. Of those that a mesh axis runs over, the one named last changes fastest.
Arguments:
- matrix_slab: float32 [32, 1048576], P(None, ('grp', 'dev')), may hold values from -6 to 6
- sign_flips: int32 [1048576], P(('grp', 'dev')), may hold values from 0 to 1
- sample_offset: int32 [4096], P(('grp', 'dev')), may hold values from 0 to 4095, as said below
Outputs:
- transformed: float32 [32, 1048576], P(None, ('grp', 'dev'))
- sketch: float32 [32, 4096], P(None, ('grp', 'dev'))
- gram_matrix: float32 [32, 32], replicated
The draws below stay inside these ranges and needn't reach their ends.
Inputs may be any that keep to these rules, and one draw needn't show every extreme that they name: Entry k selects row (k // 16) * 4096 + sample_offset[k] of the transform; rows may repeat.
All inputs are finite; a program needn't handle non-finite values.
Results may differ from the reference program's by a relative error of at most 0.00011.
Values sent between devices are 32-bit elements; how exact they have to be, the bound alone decides.
A program may use at most 64 MiB of HBM per device.

```python
import math
import jax
import jax.numpy as jnp
from jax import lax

COLS = 32
ROWS_DEV = 4096
SAMP_DEV = 16
ROWS = 1048576
SAMPLES = 4096


def draw_sample_offset(key, part):
    key = jax.random.fold_in(key, 11)
    picked = jax.random.randint(key, (SAMPLES,), 0, ROWS_DEV, dtype=jnp.int32)
    picked = picked.at[0].set(0)
    picked = picked.at[SAMPLES - 1].set(ROWS_DEV - 1)
    return picked


def plant(values, key, smallest, largest):
    shape = values.shape
    place = [jax.random.randint(jax.random.fold_in(key, axis), (), 0, shape[axis]) for axis in range(len(shape))]
    values = values.at[tuple(place)].set(smallest)
    longest = shape.index(max(shape))
    place[longest] = (place[longest] + 1) % shape[longest]
    return values.at[tuple(place)].set(largest)


def shard_levels(key, dims, pieces, low, high):
    gain, own = 1.0, jax.random.fold_in(key, 6)
    for dim, shards_of in pieces:
        heights = jnp.exp(jax.random.uniform(jax.random.fold_in(own, dim), (shards_of,), jnp.float32, low / len(pieces), high / len(pieces)))
        gain = gain * jnp.repeat(heights, dims[dim] // shards_of).reshape([-1 if axis == dim else 1 for axis in range(len(dims))])
    return gain


def centred(stream_key, shape, scale, most, pieces=(), held_as=jnp.bfloat16):
    drawn = jax.random.normal(stream_key, shape, jnp.float32) * scale
    if len(pieces) > 0:
        drawn = shard_levels(stream_key, shape, pieces, -0.22, 0.18) * drawn
    return jnp.clip(drawn, min=-most, max=most).astype(held_as)


def setup_inputs(seed: int = 0) -> dict:
    arg_keys = jax.random.split(jax.random.key(seed), 4)
    matrix_slab = centred(arg_keys[0], (COLS, ROWS), 1.0, 6.0, ((1, 256),), jnp.float32)
    sign_flips = plant(jax.random.randint(arg_keys[1], (ROWS,), 0, 2), jax.random.fold_in(arg_keys[1], 1), 0, 1).astype(jnp.int32)
    sample_offset = draw_sample_offset(jax.random.fold_in(arg_keys[3], 71), 0)
    return {"matrix_slab": matrix_slab, "sign_flips": sign_flips, "sample_offset": sample_offset}


def hadamard_table(order):
    numbers = jnp.arange(order, dtype=jnp.int32)
    common_bits = numbers[:, None] & numbers[None, :]
    parity = jnp.zeros((order, order), dtype=jnp.int32)
    for position in range(max(order.bit_length() - 1, 0)):
        parity = parity + (common_bits >> position & 1)
    return (1 - 2 * (parity % 2)).astype(jnp.float32)

def split_sizes(length):
    factors = []
    remain = length
    while remain > 1:
        factor = min(128, remain)
        factors.append(factor)
        remain = remain // factor
    return factors

def mix_last(values, length):
    leading = values.shape[:-1]
    factors = split_sizes(length)
    if len(factors) == 0:
        return values
    shaped = values.reshape(leading + tuple(factors))
    letters = 'abcdefghij'
    total = len(leading) + len(factors)
    source = letters[:total]
    for position in range(len(factors)):
        axis_at = len(leading) + position
        target = source[:axis_at] + 'z' + source[axis_at + 1:]
        shaped = jnp.einsum(source + ',z' + source[axis_at] + '->' + target, shaped, hadamard_table(factors[position]), precision=lax.Precision.HIGHEST)
    return shaped.reshape(values.shape)

def reference(matrix_slab, sign_flips, sample_offset):
    signs = (1 - 2 * sign_flips).astype(jnp.float32)
    signed = matrix_slab * signs[None, :]
    transformed = mix_last(signed, ROWS) * jnp.float32(1.0 / math.sqrt(ROWS))
    blocks = (jnp.arange(SAMPLES, dtype=jnp.int32) // SAMP_DEV).astype(jnp.int32)
    chosen = (blocks * ROWS_DEV + sample_offset).astype(jnp.int32)
    sketch = jnp.take(transformed, chosen, axis=1)
    gram_matrix = jnp.dot(sketch, sketch.T, precision=lax.Precision.HIGHEST, preferred_element_type=jnp.float32) / jnp.float32(SAMPLES)
    return (transformed, sketch, gram_matrix)
```

```python
import functools

import jax
import jax.numpy as jnp
from jax import lax
from jax.experimental import pallas as pl
from jax.experimental.pallas import tpu as pltpu
from jax.sharding import PartitionSpec as P

MESH = pl.DeviceIdType.MESH
LANES = 128
SIDE = 16
COLS = 32
LOCAL = 4096
SAMPLES = 16
TOTAL_SAMPLES = 4096
ROWS = LOCAL * COLS // LANES
SCALE = 2.0**-10
PARTS = ((0, 512, True), (512, 512, False))


def fwht(values):
    values = list(values)
    step = 1
    while step < len(values):
        for low in range(0, len(values), 2 * step):
            for at in range(low, low + step):
                a, b = values[at], values[at + step]
                values[at], values[at + step] = a + b, a - b
        step *= 2
    return values


def tree_sum(values):
    values = list(values)
    while len(values) > 1:
        values = [values[i] + values[i + 1] for i in range(0, len(values), 2)]
    return values[0]


def split(value):
    high = value.astype(jnp.bfloat16)
    low = (value - high.astype(jnp.float32)).astype(jnp.bfloat16)
    return high, low


def hadamard(order, scale):
    shape = (order, order)
    common = lax.broadcasted_iota(jnp.int32, shape, 0) & lax.broadcasted_iota(jnp.int32, shape, 1)
    shift = order // 2
    bits = order.bit_length() - 1
    parity = common & 1
    for position in range(1, bits):
        parity = parity ^ ((common >> position) & 1)
    del shift
    return jnp.where(parity == 1, -scale, scale).astype(jnp.bfloat16)


class Team:
    def __init__(self, grp, dev, along_z):
        self.along_z = along_z
        self.grp, self.high, self.low = grp, dev // 16, dev % 16
        self.me = grp + 8 * self.high if along_z else self.low

    def device(self, index):
        if self.along_z:
            return (index % 8, (index // 8) * 16 + self.low)
        return (self.grp, self.high * 16 + index)

    def peer(self, turn):
        away = (turn + 1) // 2
        return (self.me + 8 + away * (2 * ((turn + 1) % 2) - 1)) % SIDE

    def each(self, body):
        def step(turn, carry):
            body(self.peer(turn))
            return carry

        lax.fori_loop(0, SIDE - 1, step, 0)


def rows_at(index, count):
    return pl.ds(pl.multiple_of(index * count, 8), count)


def exchange(team, src, dst, sems, phase, size):
    def one(index):
        pltpu.make_async_remote_copy(
            src_ref=src.at[rows_at(index, size)],
            dst_ref=dst.at[rows_at(team.me, size)],
            send_sem=sems.at[0, phase],
            recv_sem=sems.at[1, phase],
            device_id=team.device(index),
            device_id_type=MESH,
        ).start()

    team.each(one)
    mine = rows_at(team.me, size)
    dst[mine, :] = src[mine, :]


def arrived(dst, sems, phase, size):
    block = dst.at[pl.ds(0, (SIDE - 1) * size)]
    pltpu.make_async_copy(block, block, sems.at[1, phase]).wait()


def sent(dst, sems, phase, size):
    block = dst.at[pl.ds(0, (SIDE - 1) * size)]
    pltpu.make_async_copy(block, block, sems.at[0, phase]).wait()


def mix(src, dst, size):
    def tile(at, carry):
        values = [src[pl.ds(pl.multiple_of(j * size + at * 8, 8), 8), :] for j in range(SIDE)]
        for j, value in enumerate(fwht(values)):
            dst[pl.ds(pl.multiple_of(j * size + at * 8, 8), 8), :] = value
        return carry

    lax.fori_loop(0, size // 8, tile, 0)


def to_inner(src, dst, size):
    def block(at, carry):
        for half in range(2):
            rows = src[pl.ds(at + half * 8 * size, 8, stride=size), :]
            dst[pl.ds(pl.multiple_of(at * SIDE + half * 8, 8), 8), :] = rows
        return carry

    lax.fori_loop(0, size, block, 0, unroll=8)


def to_outer(src, dst, size):
    def block(at, carry):
        for tile in range(size // 8):
            rows = src[pl.ds(at + tile * 8 * SIDE, 8, stride=SIDE), :]
            dst[pl.ds(pl.multiple_of(at * size + tile * 8, 8), 8), :] = rows
        return carry

    lax.fori_loop(0, SIDE, block, 0, unroll=4)


def gram_of(mid, part, first, outer, inner_along_z, offsets):
    start, count, _ = part
    size = count // SIDE
    lane = lax.broadcasted_iota(jnp.int32, (8, LANES), 1)
    marks = []
    for j in range(SIDE):
        for r in range(size // 16):
            row = start + first * size + outer * (size // 16) + r
            place = ((row // LANES) * 4 + lane // COLS) * LANES + row % LANES
            place = place.astype(jnp.float32)
            for half in range(2):
                if inner_along_z:
                    held = offsets[pl.ds(j * SIDE + half * 8, 8), :]
                else:
                    held = offsets[pl.ds(j + half * 8 * SIDE, 8, stride=SIDE), :]
                marks.append(jnp.where(held == place, 1.0, 0.0))
    marks = jnp.concatenate(marks, axis=0).astype(jnp.bfloat16)
    a = lax.broadcasted_iota(jnp.int32, (LANES, LANES), 0) // COLS
    b = lax.broadcasted_iota(jnp.int32, (LANES, LANES), 1) // COLS
    same = jnp.where(a == b, 1.0, 0.0).astype(jnp.bfloat16)
    counts = jnp.dot(marks, same, preferred_element_type=jnp.float32)
    values = mid[...]
    return lax.dot_general(
        values,
        counts * values,
        (((0,), (0,)), ((), ())),
        precision=lax.Precision.HIGHEST,
        preferred_element_type=jnp.float32,
    )


def kernel(x_any, flips_any, offs_any, out_any, sketch_ref, gram_ref, *scratch):
    (x, flips, offs, mixed, final, out, off_row, off_z, off_plane, off_all, gram_rows, gram_xy,
     gram_z, gram_sum, gram_all, picked, load_sems, store_sems, sems, small_sems) = scratch[:20]
    held = [scratch[20 + 8 * i : 28 + 8 * i] for i in range(len(PARTS))]
    grp, dev = lax.axis_index("grp"), lax.axis_index("dev")
    zs, xy = Team(grp, dev, True), Team(grp, dev, False)

    load_x = pltpu.make_async_copy(x_any, x, load_sems.at[0])
    load_f = pltpu.make_async_copy(flips_any, flips, load_sems.at[1])
    load_o = pltpu.make_async_copy(offs_any, offs, load_sems.at[2])
    load_x.start()
    load_f.start()
    load_o.start()

    barrier = pltpu.get_barrier_semaphore()
    for team in (zs, xy):
        team.each(
            lambda index, team=team: pl.semaphore_signal(
                barrier, inc=1, device_id=team.device(index), device_id_type=MESH
            )
        )

    table = hadamard(LANES, SCALE)
    tables = jnp.concatenate([table, table], axis=1)
    load_f.wait()
    load_x.wait()
    for group in range(COLS // 8):
        values = []
        for blk in range(LOCAL // LANES):
            sign = (1 - 2 * flips[pl.ds(blk, 1), :]).astype(jnp.float32)
            values.append(x[pl.ds(group * 8, 8), pl.ds(blk * LANES, LANES)] * sign)
        for blk, value in enumerate(fwht(values)):
            mixed[pl.ds(blk * COLS + group * 8, 8), :] = value

    def local(part, send):
        start, count, _ = part
        for at in range(0, count, LANES):
            high, low = split(mixed[pl.ds(start + at, LANES), :])
            send[pl.ds(at, LANES), :] = lax.dot_general(
                tables,
                jnp.concatenate([high, low], axis=1),
                (((1,), (1,)), ((), ())),
                preferred_element_type=jnp.float32,
            )

    def teams(i):
        return (zs, xy) if PARTS[i][2] else (xy, zs)

    def size(i):
        return PARTS[i][1] // SIDE

    def scatter_outer(i):
        local(PARTS[i], held[i][0])
        exchange(teams(i)[0], held[i][0], held[i][1], sems, 4 * i, size(i))

    def scatter_inner(i):
        _, got, flat, turned, got_inner, _, _, _ = held[i]
        arrived(got, sems, 4 * i, size(i))
        mix(got, flat, size(i))
        to_inner(flat, turned, size(i))
        exchange(teams(i)[1], turned, got_inner, sems, 4 * i + 1, size(i))

    def return_inner(i):
        got_inner, mid, back = held[i][4:7]
        arrived(got_inner, sems, 4 * i + 1, size(i))
        mix(got_inner, mid, size(i))
        exchange(teams(i)[1], mid, back, sems, 4 * i + 2, size(i))

    def return_outer(i):
        back, flat = held[i][6:8]
        arrived(back, sems, 4 * i + 2, size(i))
        to_outer(back, flat, size(i))
        mine = final.at[pl.ds(PARTS[i][0], PARTS[i][1])]
        exchange(teams(i)[0], flat, mine, sems, 4 * i + 3, size(i))

    def finish(i):
        start, count, _ = PARTS[i]
        arrived(final.at[pl.ds(start, count)], sems, 4 * i + 3, size(i))
        for at in range(start, start + count, LANES):
            block = final[pl.ds(at, LANES), :].T
            for b in range(4):
                out[:, pl.ds((at // LANES * 4 + b) * LANES, LANES)] = block[b * COLS : (b + 1) * COLS]
        columns = pl.ds(start * 4, count * 4)
        pltpu.make_async_copy(out.at[:, columns], out_any.at[:, columns], store_sems.at[i]).start()

    def small(team, index, src, dst, phase):
        pltpu.make_async_remote_copy(
            src_ref=src,
            dst_ref=dst,
            send_sem=small_sems.at[0, phase],
            recv_sem=small_sems.at[1, phase],
            device_id=team.device(index),
            device_id_type=MESH,
        ).start()

    def small_done(block, side, phase):
        pltpu.make_async_copy(block, block, small_sems.at[side, phase]).wait()

    load_o.wait()
    lane = lax.broadcasted_iota(jnp.int32, (1, LANES), 1)
    row = jnp.full((1, LANES), -1, jnp.int32)
    for k in range(SAMPLES):
        row = jnp.where(lane % COLS == k, offs[k], row)
    off_row[...] = row.astype(jnp.float32)[None]

    pl.semaphore_wait(barrier, 2 * (SIDE - 1))

    scatter_outer(0)
    scatter_outer(1)
    zs.each(lambda index: small(zs, index, off_row, off_z.at[pl.ds(zs.me, 1)], 0))
    off_z[pl.ds(zs.me, 1)] = off_row[...]
    scatter_inner(1)
    small_done(off_z.at[pl.ds(0, SIDE - 1)], 1, 0)
    for j in range(SIDE):
        off_plane[pl.ds(j, 1), :] = off_z[j]
    xy.each(lambda index: small(xy, index, off_plane, off_all.at[rows_at(xy.me, SIDE)], 1))
    off_all[rows_at(xy.me, SIDE), :] = off_plane[...]
    scatter_inner(0)
    return_inner(0)
    return_inner(1)

    small_done(off_all.at[pl.ds(0, SIDE * (SIDE - 1))], 1, 1)
    product = tree_sum(
        gram_of(held[i][5], PARTS[i], teams(i)[0].me, teams(i)[1].me, PARTS[i][2], off_all)
        for i in range(len(PARTS))
    )
    lane32 = lax.broadcasted_iota(jnp.int32, (COLS, LANES), 1) // COLS
    folded = tree_sum(
        jnp.where(lane32 == b, product[b * COLS : (b + 1) * COLS], 0.0) for b in range(4)
    )
    folded = folded + pltpu.roll(folded, 64, 1)
    folded = folded + pltpu.roll(folded, 32, 1)
    lane8 = lax.broadcasted_iota(jnp.int32, (8, LANES), 1) // COLS
    packed = tree_sum(
        jnp.where(lane8 == b, folded[b * 8 : (b + 1) * 8], 0.0) for b in range(4)
    )
    packed = packed * (1.0 / TOTAL_SAMPLES)
    for i in range(8):
        gram_rows[i] = packed[i : i + 1]
    xy.each(lambda index: small(xy, index, gram_rows.at[pl.ds(index % 8, 1)], gram_xy.at[pl.ds(xy.me, 1)], 2))
    gram_xy[pl.ds(xy.me, 1)] = gram_rows[pl.ds(xy.me % 8, 1)]

    return_outer(0)

    small_done(gram_xy.at[pl.ds(0, SIDE - 1)], 1, 2)
    gram_sum[0] = tree_sum(gram_xy[j] for j in range(SIDE))
    zs.each(lambda index: small(zs, index, gram_sum.at[pl.ds(0, 1)], gram_z.at[pl.ds(zs.me, 1)], 3))
    gram_z[pl.ds(zs.me, 1)] = gram_sum[pl.ds(0, 1)]

    return_outer(1)

    small_done(gram_z.at[pl.ds(0, SIDE - 1)], 1, 3)
    gram_sum[1] = tree_sum(gram_z[j] for j in range(SIDE))

    def share(turn, carry):
        index = (xy.me // 8) * 8 + (xy.me + turn) % 8
        small(xy, index, gram_sum.at[pl.ds(1, 1)], gram_all.at[pl.ds(xy.me % 8, 1)], 4)
        return carry

    lax.fori_loop(1, 8, share, 0)
    gram_all[pl.ds(xy.me % 8, 1)] = gram_sum[pl.ds(1, 1)]

    finish(1)
    small_done(gram_all.at[pl.ds(0, 7)], 1, 4)
    whole = jnp.concatenate([gram_all[i] for i in range(8)], axis=0)
    for b in range(4):
        turned = pltpu.roll(whole, LANES - COLS * b, 1) if b else whole
        gram_ref[pl.ds(b * 8, 8), :] = turned[:, :COLS]
    finish(0)

    for k in range(SAMPLES):
        at = offs[k]
        value = final[pl.ds((at // 512) * LANES + at % LANES, 1), :]
        picked[pl.ds(k, 1), :] = jnp.where(lane // COLS == (at // LANES) % 4, value, 0.0)
    c = lax.broadcasted_iota(jnp.int32, (COLS, LANES), 0)
    l = lax.broadcasted_iota(jnp.int32, (COLS, LANES), 1)
    sketch_ref[...] = lax.dot_general(
        jnp.where(l % COLS == c, 1.0, 0.0),
        picked[...],
        (((1,), (1,)), ((), ())),
        precision=lax.Precision.HIGHEST,
        preferred_element_type=jnp.float32,
    )

    for i in range(len(PARTS)):
        for phase in range(4):
            sent(held[i][1], sems, 4 * i + phase, size(i))
    small_done(off_z.at[pl.ds(0, SIDE - 1)], 0, 0)
    small_done(off_all.at[pl.ds(0, SIDE * (SIDE - 1))], 0, 1)
    small_done(gram_xy.at[pl.ds(0, SIDE - 1)], 0, 2)
    small_done(gram_z.at[pl.ds(0, SIDE - 1)], 0, 3)
    small_done(gram_all.at[pl.ds(0, 7)], 0, 4)
    for i in range(len(PARTS)):
        columns = pl.ds(PARTS[i][0] * 4, PARTS[i][1] * 4)
        pltpu.make_async_copy(out.at[:, columns], out_any.at[:, columns], store_sems.at[i]).wait()


def local(matrix_slab, sign_flips, sample_offset):
    f32 = jnp.float32
    scratch = [
        pltpu.VMEM((COLS, LOCAL), f32),
        pltpu.VMEM((LOCAL // LANES, LANES), jnp.int32),
        pltpu.SMEM((SAMPLES,), jnp.int32),
        pltpu.VMEM((ROWS, LANES), f32),
        pltpu.VMEM((ROWS, LANES), f32),
        pltpu.VMEM((COLS, LOCAL), f32),
        pltpu.VMEM((1, 1, LANES), f32),
        pltpu.VMEM((SIDE, 1, LANES), f32),
        pltpu.VMEM((SIDE, LANES), f32),
        pltpu.VMEM((SIDE * SIDE, LANES), f32),
        pltpu.VMEM((8, 1, LANES), f32),
        pltpu.VMEM((SIDE, 1, LANES), f32),
        pltpu.VMEM((SIDE, 1, LANES), f32),
        pltpu.VMEM((2, 1, LANES), f32),
        pltpu.VMEM((8, 1, LANES), f32),
        pltpu.VMEM((SAMPLES, LANES), f32),
        pltpu.SemaphoreType.DMA((3,)),
        pltpu.SemaphoreType.DMA((len(PARTS),)),
        pltpu.SemaphoreType.DMA((2, 4 * len(PARTS))),
        pltpu.SemaphoreType.DMA((2, 5)),
    ]
    for _, count, _ in PARTS:
        scratch += [pltpu.VMEM((count, LANES), f32)] * 8
    return pl.pallas_call(
        kernel,
        out_shape=(
            jax.ShapeDtypeStruct((COLS, LOCAL), f32),
            jax.ShapeDtypeStruct((COLS, SAMPLES), f32),
            jax.ShapeDtypeStruct((COLS, COLS), f32),
        ),
        in_specs=[pl.BlockSpec(memory_space=pl.ANY)] * 3,
        out_specs=(
            pl.BlockSpec(memory_space=pl.ANY),
            pl.BlockSpec(memory_space=pltpu.VMEM),
            pl.BlockSpec(memory_space=pltpu.VMEM),
        ),
        scratch_shapes=scratch,
        compiler_params=pltpu.CompilerParams(
            collective_id=0, has_side_effects=True, vmem_limit_bytes=24 << 20
        ),
        name="hadamard",
    )(matrix_slab, sign_flips.reshape(LOCAL // LANES, LANES), sample_offset)


def solution(mesh):
    return jax.shard_map(
        local,
        mesh=mesh,
        in_specs=(P(None, ("grp", "dev")), P(("grp", "dev")), P(("grp", "dev"))),
        out_specs=(P(None, ("grp", "dev")), P(None, ("grp", "dev")), P()),
        check_vma=False,
    )
```

```python
import functools

import jax
import jax.numpy as jnp
from jax import lax
from jax.experimental import pallas as pl
from jax.experimental.pallas import tpu as pltpu
from jax.sharding import PartitionSpec as P

MESH = pl.DeviceIdType.MESH
LANES = 128
SIDE = 16
COLS = 32
LOCAL = 4096
SAMPLES = 16
TOTAL_SAMPLES = 4096
ROWS = LOCAL * COLS // LANES
SCALE = 2.0**-10
PARTS = ((0, 256, True), (256, 256, True), (512, 256, False), (768, 256, False))


def fwht(values):
    values = list(values)
    step = 1
    while step < len(values):
        for low in range(0, len(values), 2 * step):
            for at in range(low, low + step):
                a, b = values[at], values[at + step]
                values[at], values[at + step] = a + b, a - b
        step *= 2
    return values


def tree_sum(values):
    values = list(values)
    while len(values) > 1:
        values = [values[i] + values[i + 1] for i in range(0, len(values), 2)]
    return values[0]


def split(value):
    high = value.astype(jnp.bfloat16)
    low = (value - high.astype(jnp.float32)).astype(jnp.bfloat16)
    return high, low


def hadamard(order, scale):
    shape = (order, order)
    common = lax.broadcasted_iota(jnp.int32, shape, 0) & lax.broadcasted_iota(jnp.int32, shape, 1)
    bits = order.bit_length() - 1
    parity = common & 1
    for position in range(1, bits):
        parity = parity ^ ((common >> position) & 1)
    return jnp.where(parity == 1, -scale, scale).astype(jnp.bfloat16)


class Team:
    def __init__(self, grp, dev, kind):
        self.kind = kind
        self.grp, self.high, self.low = grp, dev // 16, dev % 16
        self.z, self.core = grp // 2 + 4 * self.high, grp % 2
        self.me, self.count = {
            "z": (2 * self.z + self.core, 16),
            "xy": (self.low, 16),
            "plane": (16 * self.core + self.low, 32),
            "line": (self.z, 8),
        }[kind]

    def device(self, index):
        if self.kind == "z":
            return (index % 8, (index // 8) * 16 + self.low)
        if self.kind == "xy":
            return (self.grp, self.high * 16 + index)
        if self.kind == "plane":
            return ((self.grp // 2) * 2 + index // 16, self.high * 16 + index % 16)
        return ((index % 4) * 2 + self.core, (index // 4) * 16 + self.low)

    def peer(self, turn):
        away = (turn + 1) // 2
        return (self.me + self.count // 2 + away * (2 * ((turn + 1) % 2) - 1)) % self.count

    def each(self, body):
        def step(turn, carry):
            body(self.peer(turn))
            return carry

        lax.fori_loop(0, self.count - 1, step, 0)


def rows_at(index, count):
    return pl.ds(pl.multiple_of(index * count, 8), count)


def exchange(team, src, dst, sems, phase, size):
    def one(index):
        pltpu.make_async_remote_copy(
            src_ref=src.at[rows_at(index, size)],
            dst_ref=dst.at[rows_at(team.me, size)],
            send_sem=sems.at[0, phase],
            recv_sem=sems.at[1, phase],
            device_id=team.device(index),
            device_id_type=MESH,
        ).start()

    team.each(one)
    mine = rows_at(team.me, size)
    dst[mine, :] = src[mine, :]


def arrived(dst, sems, phase, size):
    block = dst.at[pl.ds(0, (SIDE - 1) * size)]
    pltpu.make_async_copy(block, block, sems.at[1, phase]).wait()


def sent(dst, sems, phase, size):
    block = dst.at[pl.ds(0, (SIDE - 1) * size)]
    pltpu.make_async_copy(block, block, sems.at[0, phase]).wait()


def mix(src, dst, size):
    def tile(at, carry):
        values = [src[pl.ds(pl.multiple_of(j * size + at * 8, 8), 8), :] for j in range(SIDE)]
        for j, value in enumerate(fwht(values)):
            dst[pl.ds(pl.multiple_of(j * size + at * 8, 8), 8), :] = value
        return carry

    lax.fori_loop(0, size // 8, tile, 0)


def to_inner(src, dst, size):
    def block(at, carry):
        for half in range(2):
            rows = src[pl.ds(at + half * 8 * size, 8, stride=size), :]
            dst[pl.ds(pl.multiple_of(at * SIDE + half * 8, 8), 8), :] = rows
        return carry

    lax.fori_loop(0, size, block, 0, unroll=8)


def to_outer(src, dst, size):
    def block(at, carry):
        for tile in range(size // 8):
            rows = src[pl.ds(at + tile * 8 * SIDE, 8, stride=SIDE), :]
            dst[pl.ds(pl.multiple_of(at * size + tile * 8, 8), 8), :] = rows
        return carry

    lax.fori_loop(0, SIDE, block, 0, unroll=4)


def gram_of(mid, part, first, outer, inner_along_z, offsets):
    start, count, _ = part
    size = count // SIDE
    lane = lax.broadcasted_iota(jnp.int32, (8, LANES), 1)
    marks = []
    for j in range(SIDE):
        for r in range(size // 16):
            row = start + first * size + outer * (size // 16) + r
            place = ((row // LANES) * 4 + lane // COLS) * LANES + row % LANES
            place = place.astype(jnp.float32)
            for half in range(2):
                if inner_along_z:
                    held = offsets[pl.ds(j * SIDE + half * 8, 8), :]
                else:
                    held = offsets[pl.ds(j + half * 8 * SIDE, 8, stride=SIDE), :]
                marks.append(jnp.where(held == place, 1.0, 0.0))
    marks = jnp.concatenate(marks, axis=0).astype(jnp.bfloat16)
    a = lax.broadcasted_iota(jnp.int32, (LANES, LANES), 0) // COLS
    b = lax.broadcasted_iota(jnp.int32, (LANES, LANES), 1) // COLS
    same = jnp.where(a == b, 1.0, 0.0).astype(jnp.bfloat16)
    counts = jnp.dot(marks, same, preferred_element_type=jnp.float32)
    values = mid[...]
    return lax.dot_general(
        values,
        counts * values,
        (((0,), (0,)), ((), ())),
        precision=lax.Precision.HIGHEST,
        preferred_element_type=jnp.float32,
    )


def kernel(x_any, flips_any, offs_any, out, sketch, gram, *scratch):
    (x, flips, offs, mixed, final, off_row, off_z, off_plane, off_all, packed, gram_plane,
     gram_sum, gram_line, load_sems, sems, small_sems) = scratch[:16]
    held = [scratch[16 + 8 * i : 24 + 8 * i] for i in range(len(PARTS))]
    grp, dev = lax.axis_index("grp"), lax.axis_index("dev")
    zs, xy, plane, line = (Team(grp, dev, kind) for kind in ("z", "xy", "plane", "line"))

    load_x = pltpu.make_async_copy(x_any, x, load_sems.at[0])
    load_f = pltpu.make_async_copy(flips_any, flips, load_sems.at[1])
    load_o = pltpu.make_async_copy(offs_any, offs, load_sems.at[2])
    load_f.start()
    load_x.start()
    load_o.start()

    barrier = pltpu.get_barrier_semaphore()
    for team in (zs, plane):
        team.each(
            lambda index, team=team: pl.semaphore_signal(
                barrier, inc=1, device_id=team.device(index), device_id_type=MESH
            )
        )

    def teams(i):
        return (zs, xy) if PARTS[i][2] else (xy, zs)

    def size(i):
        return PARTS[i][1] // SIDE

    def small(team, index, src, dst, phase):
        pltpu.make_async_remote_copy(
            src_ref=src,
            dst_ref=dst,
            send_sem=small_sems.at[0, phase],
            recv_sem=small_sems.at[1, phase],
            device_id=team.device(index),
            device_id_type=MESH,
        ).start()

    def small_done(block, side, phase):
        pltpu.make_async_copy(block, block, small_sems.at[side, phase]).wait()

    table = hadamard(LANES, SCALE)
    tables = jnp.concatenate([table, table], axis=1)
    load_f.wait()
    load_x.wait()
    for group in range(COLS // 8):
        values = []
        for blk in range(LOCAL // LANES):
            sign = (1 - 2 * flips[pl.ds(blk, 1), :]).astype(jnp.float32)
            values.append(x[pl.ds(group * 8, 8), pl.ds(blk * LANES, LANES)] * sign)
        for blk, value in enumerate(fwht(values)):
            mixed[pl.ds(blk * COLS + group * 8, 8), :] = value

    for i, (start, count, _) in enumerate(PARTS):
        for at in range(0, count, LANES):
            high, low = split(mixed[pl.ds(start + at, LANES), :])
            held[i][0][pl.ds(at, LANES), :] = lax.dot_general(
                tables,
                jnp.concatenate([high, low], axis=1),
                (((1,), (1,)), ((), ())),
                preferred_element_type=jnp.float32,
            )

    load_o.wait()
    lane = lax.broadcasted_iota(jnp.int32, (1, LANES), 1)
    row = jnp.full((1, LANES), -1, jnp.int32)
    for k in range(SAMPLES):
        row = jnp.where(lane % COLS == k, offs[k], row)
    off_row[...] = row.astype(jnp.float32)[None]

    pl.semaphore_wait(barrier, zs.count + plane.count - 2)

    def scatter_outer(i):
        exchange(teams(i)[0], held[i][0], held[i][1], sems, 4 * i, size(i))

    def scatter_inner(i):
        _, got, flat, turned, got_inner, _, _, _ = held[i]
        arrived(got, sems, 4 * i, size(i))
        mix(got, flat, size(i))
        to_inner(flat, turned, size(i))
        exchange(teams(i)[1], turned, got_inner, sems, 4 * i + 1, size(i))

    def return_inner(i):
        got_inner, mid, back = held[i][4:7]
        arrived(got_inner, sems, 4 * i + 1, size(i))
        mix(got_inner, mid, size(i))
        exchange(teams(i)[1], mid, back, sems, 4 * i + 2, size(i))

    def return_outer(i):
        back, flat = held[i][6:8]
        arrived(back, sems, 4 * i + 2, size(i))
        to_outer(back, flat, size(i))
        mine = final.at[pl.ds(PARTS[i][0], PARTS[i][1])]
        exchange(teams(i)[0], flat, mine, sems, 4 * i + 3, size(i))

    def finish(i):
        start, count, _ = PARTS[i]
        arrived(final.at[pl.ds(start, count)], sems, 4 * i + 3, size(i))
        for at in range(start, start + count, LANES):
            block = final[pl.ds(at, LANES), :].T
            for b in range(4):
                out[:, pl.ds((at // LANES * 4 + b) * LANES, LANES)] = block[b * COLS : (b + 1) * COLS]

    def product(i):
        return gram_of(held[i][5], PARTS[i], teams(i)[0].me, teams(i)[1].me, PARTS[i][2], off_all)

    zs.each(lambda index: small(zs, index, off_row, off_z.at[pl.ds(zs.me, 1)], 0))
    scatter_outer(0)
    scatter_outer(2)
    scatter_outer(1)
    scatter_outer(3)
    off_z[pl.ds(zs.me, 1)] = off_row[...]
    small_done(off_z.at[pl.ds(0, SIDE - 1)], 1, 0)
    for j in range(SIDE):
        off_plane[pl.ds(j, 1), :] = off_z[j]
    xy.each(lambda index: small(xy, index, off_plane, off_all.at[rows_at(xy.me, SIDE)], 1))
    off_all[rows_at(xy.me, SIDE), :] = off_plane[...]

    scatter_inner(2)
    scatter_inner(0)
    scatter_inner(3)
    scatter_inner(1)
    return_inner(0)
    return_inner(2)
    small_done(off_all.at[pl.ds(0, SIDE * (SIDE - 1))], 1, 1)
    total = product(0) + product(2)
    return_inner(1)
    return_inner(3)
    total = total + (product(1) + product(3))

    lane32 = lax.broadcasted_iota(jnp.int32, (COLS, LANES), 1) // COLS
    folded = tree_sum(
        jnp.where(lane32 == b, total[b * COLS : (b + 1) * COLS], 0.0) for b in range(4)
    )
    folded = folded + pltpu.roll(folded, 64, 1)
    folded = folded + pltpu.roll(folded, 32, 1)
    lane8 = lax.broadcasted_iota(jnp.int32, (8, LANES), 1) // COLS
    tile = tree_sum(
        jnp.where(lane8 == b, folded[b * 8 : (b + 1) * 8], 0.0) for b in range(4)
    )
    packed[...] = tile * (1.0 / TOTAL_SAMPLES)
    plane.each(lambda index: small(plane, index, packed, gram_plane.at[rows_at(plane.me, 8)], 2))
    gram_plane[rows_at(plane.me, 8), :] = packed[...]

    return_outer(0)
    return_outer(2)
    return_outer(1)

    small_done(gram_plane.at[pl.ds(0, 8 * (plane.count - 1))], 1, 2)
    gram_sum[...] = tree_sum(gram_plane[pl.ds(8 * j, 8), :] for j in range(plane.count))
    line.each(lambda index: small(line, index, gram_sum, gram_line.at[rows_at(line.me, 8)], 3))
    gram_line[rows_at(line.me, 8), :] = gram_sum[...]

    return_outer(3)
    finish(2)
    finish(0)
    finish(3)

    small_done(gram_line.at[pl.ds(0, 8 * (line.count - 1))], 1, 3)
    whole = tree_sum(gram_line[pl.ds(8 * j, 8), :] for j in range(line.count))
    for b in range(4):
        turned = pltpu.roll(whole, LANES - COLS * b, 1) if b else whole
        gram[pl.ds(b * 8, 8), :] = turned[:, :COLS]
    finish(1)

    picked = []
    for k in range(SAMPLES):
        at = offs[k]
        value = final[pl.ds((at // 512) * LANES + at % LANES, 1), :]
        picked.append(jnp.where(lane // COLS == (at // LANES) % 4, value, 0.0))
    picked = jnp.concatenate(picked, axis=0)
    picked = picked + pltpu.roll(picked, 64, 1)
    picked = picked + pltpu.roll(picked, 32, 1)
    sketch[...] = picked[:, :COLS]

    for i in range(len(PARTS)):
        for phase in range(4):
            sent(held[i][1], sems, 4 * i + phase, size(i))
    small_done(off_z.at[pl.ds(0, SIDE - 1)], 0, 0)
    small_done(off_all.at[pl.ds(0, SIDE * (SIDE - 1))], 0, 1)
    small_done(gram_plane.at[pl.ds(0, 8 * (plane.count - 1))], 0, 2)
    small_done(gram_line.at[pl.ds(0, 8 * (line.count - 1))], 0, 3)


def store(*refs):
    sems = refs[6]
    copies = []
    for i in range(3):
        copies.append(pltpu.make_async_copy(refs[i], refs[3 + i], sems.at[i]))
        copies[-1].start()
    for copy in copies:
        copy.wait()


def local(matrix_slab, sign_flips, sample_offset):
    f32 = jnp.float32
    scratch = [
        pltpu.VMEM((COLS, LOCAL), f32),
        pltpu.VMEM((LOCAL // LANES, LANES), jnp.int32),
        pltpu.SMEM((SAMPLES,), jnp.int32),
        pltpu.VMEM((ROWS, LANES), f32),
        pltpu.VMEM((ROWS, LANES), f32),
        pltpu.VMEM((1, 1, LANES), f32),
        pltpu.VMEM((SIDE, 1, LANES), f32),
        pltpu.VMEM((SIDE, LANES), f32),
        pltpu.VMEM((SIDE * SIDE, LANES), f32),
        pltpu.VMEM((8, LANES), f32),
        pltpu.VMEM((32 * 8, LANES), f32),
        pltpu.VMEM((8, LANES), f32),
        pltpu.VMEM((8 * 8, LANES), f32),
        pltpu.SemaphoreType.DMA((3,)),
        pltpu.SemaphoreType.DMA((2, 4 * len(PARTS))),
        pltpu.SemaphoreType.DMA((2, 4)),
    ]
    for _, count, _ in PARTS:
        scratch += [pltpu.VMEM((count, LANES), f32)] * 8
    shapes = (
        jax.ShapeDtypeStruct((COLS, LOCAL), f32),
        jax.ShapeDtypeStruct((SAMPLES, COLS), f32),
        jax.ShapeDtypeStruct((COLS, COLS), f32),
    )
    args = (matrix_slab, sign_flips.reshape(LOCAL // LANES, LANES), sample_offset)
    args = [pltpu.with_memory_space_constraint(arg, pltpu.HBM) for arg in args]
    results = pl.pallas_call(
        kernel,
        out_shape=shapes,
        in_specs=[pl.BlockSpec(memory_space=pl.ANY)] * 3,
        out_specs=[pl.BlockSpec(memory_space=pltpu.VMEM)] * 3,
        scratch_shapes=scratch,
        compiler_params=pltpu.CompilerParams(
            collective_id=0, has_side_effects=True, vmem_limit_bytes=24 << 20
        ),
        name="hadamard",
    )(*args)
    transformed, sketch, gram = pl.pallas_call(
        store,
        out_shape=shapes,
        in_specs=[pl.BlockSpec(memory_space=pl.ANY)] * 3,
        out_specs=[pl.BlockSpec(memory_space=pl.ANY)] * 3,
        scratch_shapes=[pltpu.SemaphoreType.DMA((3,))],
        compiler_params=pltpu.CompilerParams(vmem_limit_bytes=1 << 20),
        name="store",
    )(*(pltpu.with_memory_space_constraint(value, pltpu.VMEM) for value in results))
    return transformed, sketch.T, gram


def solution(mesh):
    return jax.shard_map(
        local,
        mesh=mesh,
        in_specs=(P(None, ("grp", "dev")), P(("grp", "dev")), P(("grp", "dev"))),
        out_specs=(P(None, ("grp", "dev")), P(None, ("grp", "dev")), P()),
        check_vma=False,
    )
```

```python
import functools

import jax
import jax.numpy as jnp
from jax import lax
from jax.experimental import pallas as pl
from jax.experimental.pallas import tpu as pltpu
from jax.sharding import PartitionSpec as P

MESH = pl.DeviceIdType.MESH
LANES = 128
SIDE = 16
COLS = 32
LOCAL = 4096
SAMPLES = 16
TOTAL_SAMPLES = 4096
ROWS = LOCAL * COLS // LANES
SCALE = 2.0**-10
PARTS = ((0, 256, True), (256, 256, True), (512, 256, False), (768, 256, False))


def fwht(values):
    values = list(values)
    step = 1
    while step < len(values):
        for low in range(0, len(values), 2 * step):
            for at in range(low, low + step):
                a, b = values[at], values[at + step]
                values[at], values[at + step] = a + b, a - b
        step *= 2
    return values


def tree_sum(values):
    values = list(values)
    while len(values) > 1:
        values = [values[i] + values[i + 1] for i in range(0, len(values), 2)]
    return values[0]


def split(value):
    high = value.astype(jnp.bfloat16)
    low = (value - high.astype(jnp.float32)).astype(jnp.bfloat16)
    return high, low


def hadamard(order, scale):
    shape = (order, order)
    common = lax.broadcasted_iota(jnp.int32, shape, 0) & lax.broadcasted_iota(jnp.int32, shape, 1)
    bits = order.bit_length() - 1
    parity = common & 1
    for position in range(1, bits):
        parity = parity ^ ((common >> position) & 1)
    return jnp.where(parity == 1, -scale, scale).astype(jnp.bfloat16)


def wrap(value, count):
    return jnp.where(value >= count, value - count, value)


class Team:
    def __init__(self, grp, dev, kind):
        self.kind = kind
        self.high, self.low = lax.div(dev, 16), lax.rem(dev, 16)
        self.grp, self.core = grp, lax.rem(grp, 2)
        self.me, self.count = {
            "z": (8 * self.high + grp, 16),
            "xy": (self.low, 16),
            "line": (4 * self.high + lax.div(grp, 2), 8),
        }[kind]

    def device(self, index):
        if self.kind == "z":
            upper = index >= 8
            return (jnp.where(upper, index - 8, index), jnp.where(upper, self.low + 16, self.low))
        if self.kind == "xy":
            return (self.grp, self.high * 16 + index)
        upper = index >= 4
        near = jnp.where(upper, index - 4, index)
        return (near * 2 + self.core, jnp.where(upper, self.low + 16, self.low))

    def each(self, body):
        def step(turn, carry):
            away = lax.div(turn + 1, 2)
            apart = self.count // 2 + away * (1 - 2 * lax.rem(turn, 2))
            body(wrap(self.me + apart, self.count))
            return carry

        lax.fori_loop(0, self.count - 1, step, 0, unroll=True)


def rows_at(index, count):
    return pl.ds(pl.multiple_of(index * count, 8), count)


def exchange(team, src, dst, sems, phase, size):
    def one(index):
        pltpu.make_async_remote_copy(
            src_ref=src.at[rows_at(index, size)],
            dst_ref=dst.at[rows_at(team.me, size)],
            send_sem=sems.at[0, phase],
            recv_sem=sems.at[1, phase],
            device_id=team.device(index),
            device_id_type=MESH,
        ).start()

    team.each(one)
    mine = rows_at(team.me, size)
    dst[mine, :] = src[mine, :]


def arrived(dst, sems, phase, size):
    block = dst.at[pl.ds(0, (SIDE - 1) * size)]
    pltpu.make_async_copy(block, block, sems.at[1, phase]).wait()


def sent(dst, sems, phase, size):
    block = dst.at[pl.ds(0, (SIDE - 1) * size)]
    pltpu.make_async_copy(block, block, sems.at[0, phase]).wait()


def mix(src, dst, size):
    def tile(at, carry):
        values = [src[pl.ds(pl.multiple_of(j * size + at * 8, 8), 8), :] for j in range(SIDE)]
        for j, value in enumerate(fwht(values)):
            dst[pl.ds(pl.multiple_of(j * size + at * 8, 8), 8), :] = value
        return carry

    lax.fori_loop(0, size // 8, tile, 0)


def to_inner(src, dst, size):
    def block(at, carry):
        for half in range(2):
            rows = src[pl.ds(at + half * 8 * size, 8, stride=size), :]
            dst[pl.ds(pl.multiple_of(at * SIDE + half * 8, 8), 8), :] = rows
        return carry

    lax.fori_loop(0, size, block, 0, unroll=8)


def to_outer(src, dst, size):
    def block(at, carry):
        for tile in range(size // 8):
            rows = src[pl.ds(at + tile * 8 * SIDE, 8, stride=SIDE), :]
            dst[pl.ds(pl.multiple_of(at * size + tile * 8, 8), 8), :] = rows
        return carry

    lax.fori_loop(0, SIDE, block, 0, unroll=4)


def gram_of(mid, part, first, outer, inner_along_z, offsets):
    start, count, _ = part
    size = count // SIDE
    lane = lax.broadcasted_iota(jnp.int32, (8, LANES), 1)
    marks = []
    for j in range(SIDE):
        for r in range(size // 16):
            row = start + first * size + outer * (size // 16) + r
            place = ((row // LANES) * 4 + lane // COLS) * LANES + row % LANES
            place = place.astype(jnp.float32)
            for half in range(2):
                if inner_along_z:
                    held = offsets[pl.ds(j * SIDE + half * 8, 8), :]
                else:
                    held = offsets[pl.ds(j + half * 8 * SIDE, 8, stride=SIDE), :]
                marks.append(jnp.where(held == place, 1.0, 0.0))
    marks = jnp.concatenate(marks, axis=0).astype(jnp.bfloat16)
    a = lax.broadcasted_iota(jnp.int32, (LANES, LANES), 0) // COLS
    b = lax.broadcasted_iota(jnp.int32, (LANES, LANES), 1) // COLS
    same = jnp.where(a == b, 1.0, 0.0).astype(jnp.bfloat16)
    counts = jnp.dot(marks, same, preferred_element_type=jnp.float32)
    values = mid[...]
    return lax.dot_general(
        values,
        counts * values,
        (((0,), (0,)), ((), ())),
        precision=lax.Precision.HIGHEST,
        preferred_element_type=jnp.float32,
    )


def kernel(x_any, flips_any, offs_any, out, sketch, gram, *scratch):
    (x, flips, offs, mixed, final, off_row, off_z, off_plane, off_all, packed, gram_xy,
     gram_core, gram_sum, gram_line, load_sems, sems, small_sems) = scratch[:17]
    held = [scratch[17 + 8 * i : 25 + 8 * i] for i in range(len(PARTS))]
    grp, dev = lax.axis_index("grp"), lax.axis_index("dev")
    zs, xy, line = (Team(grp, dev, kind) for kind in ("z", "xy", "line"))

    load_x = pltpu.make_async_copy(x_any, x, load_sems.at[0])
    load_f = pltpu.make_async_copy(flips_any, flips, load_sems.at[1])
    load_o = pltpu.make_async_copy(offs_any, offs, load_sems.at[2])
    load_f.start()
    load_x.start()
    load_o.start()

    barrier = pltpu.get_barrier_semaphore()
    for team in (xy, zs):
        team.each(
            lambda index, team=team: pl.semaphore_signal(
                barrier, inc=1, device_id=team.device(index), device_id_type=MESH
            )
        )

    def teams(i):
        return (zs, xy) if PARTS[i][2] else (xy, zs)

    def size(i):
        return PARTS[i][1] // SIDE

    def small(team, index, src, dst, phase):
        pltpu.make_async_remote_copy(
            src_ref=src,
            dst_ref=dst,
            send_sem=small_sems.at[0, phase],
            recv_sem=small_sems.at[1, phase],
            device_id=team.device(index),
            device_id_type=MESH,
        ).start()

    def small_done(block, side, phase):
        pltpu.make_async_copy(block, block, small_sems.at[side, phase]).wait()

    table = hadamard(LANES, SCALE)
    tables = jnp.concatenate([table, table], axis=1)
    load_f.wait()
    load_x.wait()
    for group in range(COLS // 8):
        values = []
        for blk in range(LOCAL // LANES):
            sign = (1 - 2 * flips[pl.ds(blk, 1), :]).astype(jnp.float32)
            values.append(x[pl.ds(group * 8, 8), pl.ds(blk * LANES, LANES)] * sign)
        for blk, value in enumerate(fwht(values)):
            mixed[pl.ds(blk * COLS + group * 8, 8), :] = value

    for i, (start, count, _) in enumerate(PARTS):
        for at in range(0, count, LANES):
            high, low = split(mixed[pl.ds(start + at, LANES), :])
            held[i][0][pl.ds(at, LANES), :] = lax.dot_general(
                tables,
                jnp.concatenate([high, low], axis=1),
                (((1,), (1,)), ((), ())),
                preferred_element_type=jnp.float32,
            )

    pl.semaphore_wait(barrier, zs.count + xy.count - 2)

    def scatter_outer(i):
        exchange(teams(i)[0], held[i][0], held[i][1], sems, 4 * i, size(i))

    def scatter_inner(i):
        _, got, flat, turned, got_inner, _, _, _ = held[i]
        arrived(got, sems, 4 * i, size(i))
        mix(got, flat, size(i))
        to_inner(flat, turned, size(i))
        exchange(teams(i)[1], turned, got_inner, sems, 4 * i + 1, size(i))

    def return_inner(i):
        got_inner, mid, back = held[i][4:7]
        arrived(got_inner, sems, 4 * i + 1, size(i))
        mix(got_inner, mid, size(i))
        exchange(teams(i)[1], mid, back, sems, 4 * i + 2, size(i))

    def return_outer(i):
        back, flat = held[i][6:8]
        arrived(back, sems, 4 * i + 2, size(i))
        to_outer(back, flat, size(i))
        mine = final.at[pl.ds(PARTS[i][0], PARTS[i][1])]
        exchange(teams(i)[0], flat, mine, sems, 4 * i + 3, size(i))

    def finish(i):
        start, count, _ = PARTS[i]
        arrived(final.at[pl.ds(start, count)], sems, 4 * i + 3, size(i))
        for at in range(start, start + count, LANES):
            block = final[pl.ds(at, LANES), :].T
            for b in range(4):
                out[:, pl.ds((at // LANES * 4 + b) * LANES, LANES)] = block[b * COLS : (b + 1) * COLS]

    def product(i):
        return gram_of(held[i][5], PARTS[i], teams(i)[0].me, teams(i)[1].me, PARTS[i][2], off_all)

    scatter_outer(0)
    scatter_outer(2)
    load_o.wait()
    lane = lax.broadcasted_iota(jnp.int32, (1, LANES), 1)
    row = jnp.full((1, LANES), -1, jnp.int32)
    for k in range(SAMPLES):
        row = jnp.where(lane % COLS == k, offs[k], row)
    off_row[...] = row.astype(jnp.float32)[None]

    zs.each(lambda index: small(zs, index, off_row, off_z.at[pl.ds(zs.me, 1)], 0))
    scatter_outer(1)
    scatter_outer(3)
    off_z[pl.ds(zs.me, 1)] = off_row[...]
    scatter_inner(2)
    scatter_inner(0)
    small_done(off_z.at[pl.ds(0, SIDE - 1)], 1, 0)
    for j in range(SIDE):
        off_plane[pl.ds(j, 1), :] = off_z[j]
    xy.each(lambda index: small(xy, index, off_plane, off_all.at[rows_at(xy.me, SIDE)], 1))
    off_all[rows_at(xy.me, SIDE), :] = off_plane[...]

    scatter_inner(3)
    scatter_inner(1)
    return_inner(2)
    return_inner(0)
    small_done(off_all.at[pl.ds(0, SIDE * (SIDE - 1))], 1, 1)
    return_inner(3)
    return_inner(1)
    total = product(0) + product(1) + product(2) + product(3)
    lane32 = lax.broadcasted_iota(jnp.int32, (COLS, LANES), 1) // COLS
    folded = tree_sum(
        jnp.where(lane32 == b, total[b * COLS : (b + 1) * COLS], 0.0) for b in range(4)
    )
    folded = folded + pltpu.roll(folded, 64, 1)
    folded = folded + pltpu.roll(folded, 32, 1)
    lane8 = lax.broadcasted_iota(jnp.int32, (8, LANES), 1) // COLS
    tile = tree_sum(
        jnp.where(lane8 == b, folded[b * 8 : (b + 1) * 8], 0.0) for b in range(4)
    )
    packed[...] = tile * (1.0 / TOTAL_SAMPLES)
    xy.each(lambda index: small(xy, index, packed, gram_xy.at[rows_at(xy.me, 8)], 2))
    gram_xy[rows_at(xy.me, 8), :] = packed[...]

    return_outer(0)
    return_outer(2)
    small_done(gram_xy.at[pl.ds(0, 8 * (xy.count - 1))], 1, 2)
    gram_core[pl.ds(0, 8), :] = tree_sum(gram_xy[pl.ds(8 * j, 8), :] for j in range(xy.count))
    small(zs, zs.me + 1 - 2 * zs.core, gram_core.at[pl.ds(0, 8)], gram_core.at[pl.ds(8, 8)], 3)

    return_outer(1)
    small_done(gram_core.at[pl.ds(8, 8)], 1, 3)
    gram_sum[...] = gram_core[pl.ds(0, 8), :] + gram_core[pl.ds(8, 8), :]
    line.each(lambda index: small(line, index, gram_sum, gram_line.at[rows_at(line.me, 8)], 4))
    gram_line[rows_at(line.me, 8), :] = gram_sum[...]

    return_outer(3)
    finish(2)
    finish(0)
    finish(3)
    for i in range(len(PARTS)):
        for phase in range(3):
            sent(held[i][1], sems, 4 * i + phase, size(i))
    small_done(gram_line.at[pl.ds(0, 8 * (line.count - 1))], 1, 4)
    whole = tree_sum(gram_line[pl.ds(8 * j, 8), :] for j in range(line.count))
    for b in range(4):
        turned = pltpu.roll(whole, LANES - COLS * b, 1) if b else whole
        gram[pl.ds(b * 8, 8), :] = turned[:, :COLS]
    finish(1)

    picked = []
    for k in range(SAMPLES):
        at = offs[k]
        value = final[pl.ds((at // 512) * LANES + at % LANES, 1), :]
        picked.append(jnp.where(lane // COLS == (at // LANES) % 4, value, 0.0))
    picked = jnp.concatenate(picked, axis=0)
    picked = picked + pltpu.roll(picked, 64, 1)
    picked = picked + pltpu.roll(picked, 32, 1)
    sketch[...] = picked[:, :COLS]

    for i in range(len(PARTS)):
        sent(held[i][1], sems, 4 * i + 3, size(i))
    small_done(off_z.at[pl.ds(0, SIDE - 1)], 0, 0)
    small_done(off_all.at[pl.ds(0, SIDE * (SIDE - 1))], 0, 1)
    small_done(gram_xy.at[pl.ds(0, 8 * (xy.count - 1))], 0, 2)
    small_done(gram_core.at[pl.ds(8, 8)], 0, 3)
    small_done(gram_line.at[pl.ds(0, 8 * (line.count - 1))], 0, 4)


def store(*refs):
    sems = refs[6]
    copies = []
    for i in range(3):
        copies.append(pltpu.make_async_copy(refs[i], refs[3 + i], sems.at[i]))
        copies[-1].start()
    for copy in copies:
        copy.wait()


def local(matrix_slab, sign_flips, sample_offset):
    f32 = jnp.float32
    scratch = [
        pltpu.VMEM((COLS, LOCAL), f32),
        pltpu.VMEM((LOCAL // LANES, LANES), jnp.int32),
        pltpu.SMEM((SAMPLES,), jnp.int32),
        pltpu.VMEM((ROWS, LANES), f32),
        pltpu.VMEM((ROWS, LANES), f32),
        pltpu.VMEM((1, 1, LANES), f32),
        pltpu.VMEM((SIDE, 1, LANES), f32),
        pltpu.VMEM((SIDE, LANES), f32),
        pltpu.VMEM((SIDE * SIDE, LANES), f32),
        pltpu.VMEM((8, LANES), f32),
        pltpu.VMEM((SIDE * 8, LANES), f32),
        pltpu.VMEM((2 * 8, LANES), f32),
        pltpu.VMEM((8, LANES), f32),
        pltpu.VMEM((8 * 8, LANES), f32),
        pltpu.SemaphoreType.DMA((3,)),
        pltpu.SemaphoreType.DMA((2, 4 * len(PARTS))),
        pltpu.SemaphoreType.DMA((2, 5)),
    ]
    for _, count, _ in PARTS:
        scratch += [pltpu.VMEM((count, LANES), f32)] * 8
    shapes = (
        jax.ShapeDtypeStruct((COLS, LOCAL), f32),
        jax.ShapeDtypeStruct((SAMPLES, COLS), f32),
        jax.ShapeDtypeStruct((COLS, COLS), f32),
    )
    args = (matrix_slab, sign_flips.reshape(LOCAL // LANES, LANES), sample_offset)
    args = [pltpu.with_memory_space_constraint(arg, pltpu.HBM) for arg in args]
    results = pl.pallas_call(
        kernel,
        out_shape=shapes,
        in_specs=[pl.BlockSpec(memory_space=pl.ANY)] * 3,
        out_specs=[pl.BlockSpec(memory_space=pltpu.VMEM)] * 3,
        scratch_shapes=scratch,
        compiler_params=pltpu.CompilerParams(
            collective_id=0, has_side_effects=True, vmem_limit_bytes=24 << 20
        ),
        name="hadamard",
    )(*args)
    transformed, sketch, gram = pl.pallas_call(
        store,
        out_shape=shapes,
        in_specs=[pl.BlockSpec(memory_space=pl.ANY)] * 3,
        out_specs=[pl.BlockSpec(memory_space=pl.ANY)] * 3,
        scratch_shapes=[pltpu.SemaphoreType.DMA((3,))],
        compiler_params=pltpu.CompilerParams(vmem_limit_bytes=1 << 20),
        name="store",
    )(*(pltpu.with_memory_space_constraint(value, pltpu.VMEM) for value in results))
    return transformed, sketch.T, gram


def solution(mesh):
    return jax.shard_map(
        local,
        mesh=mesh,
        in_specs=(P(None, ("grp", "dev")), P(("grp", "dev")), P(("grp", "dev"))),
        out_specs=(P(None, ("grp", "dev")), P(None, ("grp", "dev")), P()),
        check_vma=False,
    )
```

```python
import functools

import jax
import jax.numpy as jnp
from jax import lax
from jax.experimental import pallas as pl
from jax.experimental.pallas import tpu as pltpu
from jax.sharding import PartitionSpec as P

MESH = pl.DeviceIdType.MESH
LANES = 128
SIDE = 16
COLS = 32
LOCAL = 4096
SAMPLES = 16
TOTAL_SAMPLES = 4096
ROWS = LOCAL * COLS // LANES
SCALE = 2.0**-10
PARTS = ((0, 256, True), (256, 256, True), (512, 256, False), (768, 256, False))


def fwht(values):
    values = list(values)
    step = 1
    while step < len(values):
        for low in range(0, len(values), 2 * step):
            for at in range(low, low + step):
                a, b = values[at], values[at + step]
                values[at], values[at + step] = a + b, a - b
        step *= 2
    return values


def tree_sum(values):
    values = list(values)
    while len(values) > 1:
        values = [values[i] + values[i + 1] for i in range(0, len(values), 2)]
    return values[0]


def split(value):
    high = value.astype(jnp.bfloat16)
    low = (value - high.astype(jnp.float32)).astype(jnp.bfloat16)
    return high, low


def hadamard(order, scale):
    shape = (order, order)
    common = lax.broadcasted_iota(jnp.int32, shape, 0) & lax.broadcasted_iota(jnp.int32, shape, 1)
    bits = order.bit_length() - 1
    parity = common & 1
    for position in range(1, bits):
        parity = parity ^ ((common >> position) & 1)
    return jnp.where(parity == 1, -scale, scale).astype(jnp.bfloat16)


def wrap(value, count):
    return jnp.where(value >= count, value - count, value)


class Team:
    def __init__(self, grp, dev, kind):
        self.kind = kind
        self.high, self.low = lax.div(dev, 16), lax.rem(dev, 16)
        self.grp, self.core = grp, lax.rem(grp, 2)
        self.me, self.count = {
            "z": (8 * self.high + grp, 16),
            "xy": (self.low, 16),
            "line": (4 * self.high + lax.div(grp, 2), 8),
        }[kind]

    def device(self, index):
        if self.kind == "z":
            upper = index >= 8
            return (jnp.where(upper, index - 8, index), jnp.where(upper, self.low + 16, self.low))
        if self.kind == "xy":
            return (self.grp, self.high * 16 + index)
        upper = index >= 4
        near = jnp.where(upper, index - 4, index)
        return (near * 2 + self.core, jnp.where(upper, self.low + 16, self.low))

    def partner(self, turn):
        away = lax.div(turn + 1, 2)
        apart = self.count // 2 + away * (1 - 2 * lax.rem(turn, 2))
        return wrap(self.me + apart, self.count)

    def ranked(self, turn):
        index = jnp.where(turn < 8, turn + 1 - 2 * lax.rem(turn, 2), 23 - turn)
        return jnp.where(self.me == index, 8, index)

    def each(self, body):
        def step(turn, carry):
            body(self.partner(turn))
            return carry

        lax.fori_loop(0, self.count - 1, step, 0, unroll=True)


def rows_at(index, count):
    return pl.ds(pl.multiple_of(index * count, 8), count)


def exchange(sems, *jobs):
    def step(turn, carry):
        for team, src, dst, phase, size, ranked in jobs:
            index = team.ranked(turn) if ranked else team.partner(turn)
            pltpu.make_async_remote_copy(
                src_ref=src.at[rows_at(index, size)],
                dst_ref=dst.at[rows_at(team.me, size)],
                send_sem=sems.at[0, phase],
                recv_sem=sems.at[1, phase],
                device_id=team.device(index),
                device_id_type=MESH,
            ).start()
        return carry

    lax.fori_loop(0, SIDE - 1, step, 0, unroll=True)
    for team, src, dst, phase, size, _ in jobs:
        mine = rows_at(team.me, size)
        dst[mine, :] = src[mine, :]


def arrived(dst, sems, phase, size):
    block = dst.at[pl.ds(0, (SIDE - 1) * size)]
    pltpu.make_async_copy(block, block, sems.at[1, phase]).wait()


def sent(dst, sems, phase, size):
    block = dst.at[pl.ds(0, (SIDE - 1) * size)]
    pltpu.make_async_copy(block, block, sems.at[0, phase]).wait()


def mix(src, dst, size):
    def tile(at, carry):
        values = [src[pl.ds(pl.multiple_of(j * size + at * 8, 8), 8), :] for j in range(SIDE)]
        for j, value in enumerate(fwht(values)):
            dst[pl.ds(pl.multiple_of(j * size + at * 8, 8), 8), :] = value
        return carry

    lax.fori_loop(0, size // 8, tile, 0)


def to_inner(src, dst, size):
    def block(at, carry):
        for half in range(2):
            rows = src[pl.ds(at + half * 8 * size, 8, stride=size), :]
            dst[pl.ds(pl.multiple_of(at * SIDE + half * 8, 8), 8), :] = rows
        return carry

    lax.fori_loop(0, size, block, 0, unroll=8)


def to_outer(src, dst, size):
    def block(at, carry):
        for tile in range(size // 8):
            rows = src[pl.ds(at + tile * 8 * SIDE, 8, stride=SIDE), :]
            dst[pl.ds(pl.multiple_of(at * size + tile * 8, 8), 8), :] = rows
        return carry

    lax.fori_loop(0, SIDE, block, 0, unroll=4)


def gram_of(mid, part, first, outer, inner_along_z, offsets):
    start, count, _ = part
    size = count // SIDE
    marks = [[] for _ in range(4)]
    for j in range(SIDE):
        for r in range(size // 16):
            row = start + first * size + outer * (size // 16) + r
            place = lax.div(row, LANES) * 4 * LANES + lax.rem(row, LANES)
            for half in range(2):
                if inner_along_z:
                    held = offsets[pl.ds(j * SIDE + half * 8, 8), :]
                else:
                    held = offsets[pl.ds(j + half * 8 * SIDE, 8, stride=SIDE), :]
                for b in range(4):
                    here = held == (place + b * LANES).astype(jnp.float32)
                    marks[b].append(jnp.where(here, 1.0, 0.0))
    marks = jnp.concatenate([jnp.concatenate(m, axis=0) for m in marks], axis=1)
    a = lax.broadcasted_iota(jnp.int32, (4 * LANES, LANES), 0) // LANES
    b = lax.broadcasted_iota(jnp.int32, (4 * LANES, LANES), 1) // COLS
    spread = jnp.where(a == b, 1.0, 0.0).astype(jnp.bfloat16)
    counts = jnp.dot(marks.astype(jnp.bfloat16), spread, preferred_element_type=jnp.float32)
    values = mid[...]
    return lax.dot_general(
        values,
        counts * values,
        (((0,), (0,)), ((), ())),
        precision=lax.Precision.HIGHEST,
        preferred_element_type=jnp.float32,
    )


def kernel(x_any, flips_any, offs_any, out, sketch, gram, *scratch):
    (x, flips, offs, mixed, final, off_row, off_z, off_plane, off_pairs, off_all, packed, gram_xy,
     gram_core, gram_sum, gram_line, load_sems, sems, small_sems) = scratch[:18]
    held = [scratch[18 + 8 * i : 26 + 8 * i] for i in range(len(PARTS))]
    grp, dev = lax.axis_index("grp"), lax.axis_index("dev")
    zs, xy, line = (Team(grp, dev, kind) for kind in ("z", "xy", "line"))

    load_x = pltpu.make_async_copy(x_any, x, load_sems.at[0])
    load_f = pltpu.make_async_copy(flips_any, flips, load_sems.at[1])
    load_o = pltpu.make_async_copy(offs_any, offs, load_sems.at[2])
    barrier = pltpu.get_barrier_semaphore()
    for team in (xy, zs):
        if team is zs:
            load_f.start()
            load_x.start()
            load_o.start()
        team.each(
            lambda index, team=team: pl.semaphore_signal(
                barrier, inc=1, device_id=team.device(index), device_id_type=MESH
            )
        )

    def teams(i):
        return (zs, xy) if PARTS[i][2] else (xy, zs)

    def size(i):
        return PARTS[i][1] // SIDE

    def small(team, index, src, dst, phase):
        pltpu.make_async_remote_copy(
            src_ref=src,
            dst_ref=dst,
            send_sem=small_sems.at[0, phase],
            recv_sem=small_sems.at[1, phase],
            device_id=team.device(index),
            device_id_type=MESH,
        ).start()

    def small_done(block, side, phase):
        pltpu.make_async_copy(block, block, small_sems.at[side, phase]).wait()

    table = hadamard(LANES, SCALE)
    tables = jnp.concatenate([table, table], axis=1)
    load_f.wait()
    load_x.wait()
    for group in range(COLS // 8):
        values = []
        for blk in range(LOCAL // LANES):
            sign = (1 - 2 * flips[pl.ds(blk, 1), :]).astype(jnp.float32)
            values.append(x[pl.ds(group * 8, 8), pl.ds(blk * LANES, LANES)] * sign)
        for blk, value in enumerate(fwht(values)):
            mixed[pl.ds(blk * COLS + group * 8, 8), :] = value

    for i, (start, count, _) in enumerate(PARTS):
        for at in range(0, count, LANES):
            high, low = split(mixed[pl.ds(start + at, LANES), :])
            held[i][0][pl.ds(at, LANES), :] = lax.dot_general(
                tables,
                jnp.concatenate([high, low], axis=1),
                (((1,), (1,)), ((), ())),
                preferred_element_type=jnp.float32,
            )

    pl.semaphore_wait(barrier, zs.count + xy.count - 2)

    def scatter_outer(i):
        return teams(i)[0], held[i][0], held[i][1], 4 * i, size(i), False

    def scatter_inner(i):
        _, got, flat, turned, got_inner, _, _, _ = held[i]
        arrived(got, sems, 4 * i, size(i))
        mix(got, flat, size(i))
        to_inner(flat, turned, size(i))
        return teams(i)[1], turned, got_inner, 4 * i + 1, size(i), False

    def return_inner(i):
        got_inner, mid, back = held[i][4:7]
        arrived(got_inner, sems, 4 * i + 1, size(i))
        mix(got_inner, mid, size(i))
        return teams(i)[1], mid, back, 4 * i + 2, size(i), False

    def return_outer(i):
        back, flat = held[i][6:8]
        arrived(back, sems, 4 * i + 2, size(i))
        to_outer(back, flat, size(i))
        mine = final.at[pl.ds(PARTS[i][0], PARTS[i][1])]
        return teams(i)[0], flat, mine, 4 * i + 3, size(i), PARTS[i][2]

    def finish(i):
        start, count, _ = PARTS[i]
        arrived(final.at[pl.ds(start, count)], sems, 4 * i + 3, size(i))
        for at in range(start, start + count, LANES):
            block = final[pl.ds(at, LANES), :].T
            for b in range(4):
                out[:, pl.ds((at // LANES * 4 + b) * LANES, LANES)] = block[b * COLS : (b + 1) * COLS]

    def product(i):
        return gram_of(held[i][5], PARTS[i], teams(i)[0].me, teams(i)[1].me, PARTS[i][2], off_all)

    exchange(sems, scatter_outer(0), scatter_outer(2))
    load_o.wait()
    lane = lax.broadcasted_iota(jnp.int32, (1, LANES), 1)
    row = jnp.zeros((1, LANES), jnp.int32)
    for k in range(SAMPLES):
        row = jnp.where(lane == k, offs[k], row)
    off_row[...] = row.astype(jnp.float32)[None]

    zs.each(lambda index: small(zs, index, off_row, off_z.at[pl.ds(zs.me, 1)], 0))
    off_z[pl.ds(zs.me, 1)] = off_row[...]
    exchange(sems, scatter_outer(1), scatter_outer(3))
    exchange(sems, scatter_inner(2))
    exchange(sems, scatter_inner(0))
    small_done(off_z.at[pl.ds(0, SIDE - 1)], 1, 0)
    for h in range(2):
        off_plane[0, pl.ds(h, 1), :] = tree_sum(
            pltpu.roll(off_z[8 * h + s], SAMPLES * s, 1) if s else off_z[8 * h] for s in range(8)
        )
    xy.each(lambda index: small(xy, index, off_plane, off_pairs.at[pl.ds(xy.me, 1)], 1))
    off_pairs[pl.ds(xy.me, 1)] = off_plane[...]
    exchange(sems, scatter_inner(3))
    exchange(sems, scatter_inner(1))
    exchange(sems, return_inner(2))
    exchange(sems, return_inner(0))
    exchange(sems, return_inner(3))
    exchange(sems, return_inner(1))
    small_done(off_pairs.at[pl.ds(0, SIDE - 1)], 1, 1)
    own = lax.broadcasted_iota(jnp.int32, (8, LANES), 1) // SAMPLES
    own = own == lax.broadcasted_iota(jnp.int32, (8, LANES), 0)
    for j in range(SIDE):
        for h in range(2):
            value = jnp.broadcast_to(off_pairs[j, pl.ds(h, 1), :], (8, LANES))
            off_all[pl.ds(j * SIDE + h * 8, 8), :] = jnp.where(own, value, -1.0)
    total = (product(0) + product(1)) + (product(2) + product(3))
    lane32 = lax.broadcasted_iota(jnp.int32, (COLS, LANES), 1) // COLS
    folded = tree_sum(
        jnp.where(lane32 == b, total[b * COLS : (b + 1) * COLS], 0.0) for b in range(4)
    )
    folded = folded + pltpu.roll(folded, 64, 1)
    folded = folded + pltpu.roll(folded, 32, 1)
    lane8 = lax.broadcasted_iota(jnp.int32, (8, LANES), 1) // COLS
    tile = tree_sum(
        jnp.where(lane8 == b, folded[b * 8 : (b + 1) * 8], 0.0) for b in range(4)
    )
    packed[...] = tile * (1.0 / TOTAL_SAMPLES)
    xy.each(lambda index: small(xy, index, packed, gram_xy.at[rows_at(xy.me, 8)], 2))
    gram_xy[rows_at(xy.me, 8), :] = packed[...]

    exchange(sems, return_outer(0))
    exchange(sems, return_outer(2))
    small_done(gram_xy.at[pl.ds(0, 8 * (xy.count - 1))], 1, 2)
    gram_core[pl.ds(0, 8), :] = tree_sum(gram_xy[pl.ds(8 * j, 8), :] for j in range(xy.count))
    small(zs, zs.me + 1 - 2 * zs.core, gram_core.at[pl.ds(0, 8)], gram_core.at[pl.ds(8, 8)], 3)

    exchange(sems, return_outer(1))
    small_done(gram_core.at[pl.ds(8, 8)], 1, 3)
    gram_sum[...] = gram_core[pl.ds(0, 8), :] + gram_core[pl.ds(8, 8), :]
    line.each(lambda index: small(line, index, gram_sum, gram_line.at[rows_at(line.me, 8)], 4))
    gram_line[rows_at(line.me, 8), :] = gram_sum[...]

    exchange(sems, return_outer(3))
    finish(2)
    finish(0)
    finish(3)
    for i in range(len(PARTS)):
        for phase in range(3):
            sent(held[i][1], sems, 4 * i + phase, size(i))
    small_done(gram_line.at[pl.ds(0, 8 * (line.count - 1))], 1, 4)
    whole = tree_sum(gram_line[pl.ds(8 * j, 8), :] for j in range(line.count))
    for b in range(4):
        turned = pltpu.roll(whole, LANES - COLS * b, 1) if b else whole
        gram[pl.ds(b * 8, 8), :] = turned[:, :COLS]
    finish(1)

    picked = []
    for k in range(SAMPLES):
        at = offs[k]
        value = final[pl.ds((at // 512) * LANES + at % LANES, 1), :]
        picked.append(jnp.where(lane // COLS == (at // LANES) % 4, value, 0.0))
    picked = jnp.concatenate(picked, axis=0)
    picked = picked + pltpu.roll(picked, 64, 1)
    picked = picked + pltpu.roll(picked, 32, 1)
    sketch[...] = picked[:, :COLS]

    for i in range(len(PARTS)):
        sent(held[i][1], sems, 4 * i + 3, size(i))
    small_done(off_z.at[pl.ds(0, SIDE - 1)], 0, 0)
    small_done(off_pairs.at[pl.ds(0, SIDE - 1)], 0, 1)
    small_done(gram_xy.at[pl.ds(0, 8 * (xy.count - 1))], 0, 2)
    small_done(gram_core.at[pl.ds(8, 8)], 0, 3)
    small_done(gram_line.at[pl.ds(0, 8 * (line.count - 1))], 0, 4)


def store(*refs):
    sems = refs[6]
    copies = []
    for i in range(3):
        copies.append(pltpu.make_async_copy(refs[i], refs[3 + i], sems.at[i]))
        copies[-1].start()
    for copy in copies:
        copy.wait()


def local(matrix_slab, sign_flips, sample_offset):
    f32 = jnp.float32
    scratch = [
        pltpu.VMEM((COLS, LOCAL), f32),
        pltpu.VMEM((LOCAL // LANES, LANES), jnp.int32),
        pltpu.SMEM((SAMPLES,), jnp.int32),
        pltpu.VMEM((ROWS, LANES), f32),
        pltpu.VMEM((ROWS, LANES), f32),
        pltpu.VMEM((1, 1, LANES), f32),
        pltpu.VMEM((SIDE, 1, LANES), f32),
        pltpu.VMEM((1, 2, LANES), f32),
        pltpu.VMEM((SIDE, 2, LANES), f32),
        pltpu.VMEM((SIDE * SIDE, LANES), f32),
        pltpu.VMEM((8, LANES), f32),
        pltpu.VMEM((SIDE * 8, LANES), f32),
        pltpu.VMEM((2 * 8, LANES), f32),
        pltpu.VMEM((8, LANES), f32),
        pltpu.VMEM((8 * 8, LANES), f32),
        pltpu.SemaphoreType.DMA((3,)),
        pltpu.SemaphoreType.DMA((2, 4 * len(PARTS))),
        pltpu.SemaphoreType.DMA((2, 5)),
    ]
    for _, count, _ in PARTS:
        scratch += [pltpu.VMEM((count, LANES), f32)] * 8
    shapes = (
        jax.ShapeDtypeStruct((COLS, LOCAL), f32),
        jax.ShapeDtypeStruct((SAMPLES, COLS), f32),
        jax.ShapeDtypeStruct((COLS, COLS), f32),
    )
    args = (matrix_slab, sign_flips.reshape(LOCAL // LANES, LANES), sample_offset)
    args = [pltpu.with_memory_space_constraint(arg, pltpu.HBM) for arg in args]
    results = pl.pallas_call(
        kernel,
        out_shape=shapes,
        in_specs=[pl.BlockSpec(memory_space=pl.ANY)] * 3,
        out_specs=[pl.BlockSpec(memory_space=pltpu.VMEM)] * 3,
        scratch_shapes=scratch,
        compiler_params=pltpu.CompilerParams(
            collective_id=0, has_side_effects=True, vmem_limit_bytes=24 << 20
        ),
        name="hadamard",
    )(*args)
    transformed, sketch, gram = pl.pallas_call(
        store,
        out_shape=shapes,
        in_specs=[pl.BlockSpec(memory_space=pl.ANY)] * 3,
        out_specs=[pl.BlockSpec(memory_space=pl.ANY)] * 3,
        scratch_shapes=[pltpu.SemaphoreType.DMA((3,))],
        compiler_params=pltpu.CompilerParams(vmem_limit_bytes=1 << 20),
        name="store",
    )(*(pltpu.with_memory_space_constraint(value, pltpu.VMEM) for value in results))
    return transformed, sketch.T, gram


def solution(mesh):
    return jax.shard_map(
        local,
        mesh=mesh,
        in_specs=(P(None, ("grp", "dev")), P(("grp", "dev")), P(("grp", "dev"))),
        out_specs=(P(None, ("grp", "dev")), P(None, ("grp", "dev")), P()),
        check_vma=False,
    )
```

```python
import functools

import jax
import jax.numpy as jnp
from jax import lax
from jax.experimental import pallas as pl
from jax.experimental.pallas import tpu as pltpu
from jax.sharding import PartitionSpec as P

MESH = pl.DeviceIdType.MESH
LANES = 128
SIDE = 16
COLS = 32
LOCAL = 4096
SAMPLES = 16
TOTAL_SAMPLES = 4096
ROWS = LOCAL * COLS // LANES
SCALE = 2.0**-10
PARTS = ((0, 256, True), (256, 256, True), (512, 256, False), (768, 256, False))


def fwht(values):
    values = list(values)
    step = 1
    while step < len(values):
        for low in range(0, len(values), 2 * step):
            for at in range(low, low + step):
                a, b = values[at], values[at + step]
                values[at], values[at + step] = a + b, a - b
        step *= 2
    return values


def tree_sum(values):
    values = list(values)
    while len(values) > 1:
        values = [values[i] + values[i + 1] for i in range(0, len(values), 2)]
    return values[0]


def split(value):
    high = value.astype(jnp.bfloat16)
    low = (value - high.astype(jnp.float32)).astype(jnp.bfloat16)
    return high, low


def hadamard(order, scale):
    shape = (order, order)
    common = lax.broadcasted_iota(jnp.int32, shape, 0) & lax.broadcasted_iota(jnp.int32, shape, 1)
    bits = order.bit_length() - 1
    parity = common & 1
    for position in range(1, bits):
        parity = parity ^ ((common >> position) & 1)
    return jnp.where(parity == 1, -scale, scale).astype(jnp.bfloat16)


def wrap(value, count):
    return jnp.where(value >= count, value - count, value)


class Team:
    def __init__(self, grp, dev, kind):
        self.kind = kind
        self.high, self.low = lax.div(dev, 16), lax.rem(dev, 16)
        self.grp, self.core = grp, lax.rem(grp, 2)
        self.me, self.count = {
            "z": (8 * self.high + grp, 16),
            "xy": (self.low, 16),
            "line": (4 * self.high + lax.div(grp, 2), 8),
        }[kind]

    def device(self, index):
        if self.kind == "z":
            upper = index >= 8
            return (jnp.where(upper, index - 8, index), jnp.where(upper, self.low + 16, self.low))
        if self.kind == "xy":
            return (self.grp, self.high * 16 + index)
        upper = index >= 4
        near = jnp.where(upper, index - 4, index)
        return (near * 2 + self.core, jnp.where(upper, self.low + 16, self.low))

    def partner(self, turn):
        away = lax.div(turn + 1, 2)
        apart = self.count // 2 + away * (1 - 2 * lax.rem(turn, 2))
        return wrap(self.me + apart, self.count)

    def ranked(self, turn):
        index = jnp.where(turn < 8, turn + 1 - 2 * lax.rem(turn, 2), 23 - turn)
        return jnp.where(self.me == index, 8, index)

    def each(self, body):
        def step(turn, carry):
            body(self.partner(turn))
            return carry

        lax.fori_loop(0, self.count - 1, step, 0, unroll=True)


def rows_at(index, count):
    return pl.ds(pl.multiple_of(index * count, 8), count)


def exchange(sems, *jobs):
    def step(turn, carry):
        for team, src, dst, phase, size, ranked in jobs:
            index = team.ranked(turn) if ranked else team.partner(turn)
            pltpu.make_async_remote_copy(
                src_ref=src.at[rows_at(index, size)],
                dst_ref=dst.at[rows_at(team.me, size)],
                send_sem=sems.at[0, phase],
                recv_sem=sems.at[1, phase],
                device_id=team.device(index),
                device_id_type=MESH,
            ).start()
        return carry

    lax.fori_loop(0, SIDE - 1, step, 0, unroll=True)
    for team, src, dst, phase, size, _ in jobs:
        mine = rows_at(team.me, size)
        dst[mine, :] = src[mine, :]


def arrived(dst, sems, phase, size):
    block = dst.at[pl.ds(0, (SIDE - 1) * size)]
    pltpu.make_async_copy(block, block, sems.at[1, phase]).wait()


def sent(dst, sems, phase, size):
    block = dst.at[pl.ds(0, (SIDE - 1) * size)]
    pltpu.make_async_copy(block, block, sems.at[0, phase]).wait()


def mix(src, dst, size):
    def tile(at, carry):
        values = [src[pl.ds(pl.multiple_of(j * size + at * 8, 8), 8), :] for j in range(SIDE)]
        for j, value in enumerate(fwht(values)):
            dst[pl.ds(pl.multiple_of(j * size + at * 8, 8), 8), :] = value
        return carry

    lax.fori_loop(0, size // 8, tile, 0)


def to_inner(src, dst, size):
    def block(at, carry):
        for half in range(2):
            rows = src[pl.ds(at + half * 8 * size, 8, stride=size), :]
            dst[pl.ds(pl.multiple_of(at * SIDE + half * 8, 8), 8), :] = rows
        return carry

    lax.fori_loop(0, size, block, 0, unroll=8)


def to_outer(src, dst, size):
    def block(at, carry):
        for tile in range(size // 8):
            rows = src[pl.ds(at + tile * 8 * SIDE, 8, stride=SIDE), :]
            dst[pl.ds(pl.multiple_of(at * size + tile * 8, 8), 8), :] = rows
        return carry

    lax.fori_loop(0, SIDE, block, 0, unroll=4)


def gram_of(mid, part, first, outer, inner_along_z, offsets):
    start, count, _ = part
    size = count // SIDE
    marks = [[] for _ in range(4)]
    for j in range(SIDE):
        for r in range(size // 16):
            row = start + first * size + outer * (size // 16) + r
            place = lax.div(row, LANES) * 4 * LANES + lax.rem(row, LANES)
            for half in range(2):
                if inner_along_z:
                    held = offsets[pl.ds(j * SIDE + half * 8, 8), :]
                else:
                    held = offsets[pl.ds(j + half * 8 * SIDE, 8, stride=SIDE), :]
                for b in range(4):
                    here = held == (place + b * LANES).astype(jnp.float32)
                    marks[b].append(jnp.where(here, 1.0, 0.0))
    marks = jnp.concatenate([jnp.concatenate(m, axis=0) for m in marks], axis=1)
    a = lax.broadcasted_iota(jnp.int32, (4 * LANES, LANES), 0) // LANES
    b = lax.broadcasted_iota(jnp.int32, (4 * LANES, LANES), 1) // COLS
    spread = jnp.where(a == b, 1.0, 0.0).astype(jnp.bfloat16)
    counts = jnp.dot(marks.astype(jnp.bfloat16), spread, preferred_element_type=jnp.float32)
    values = mid[...]
    return lax.dot_general(
        values,
        counts * values,
        (((0,), (0,)), ((), ())),
        precision=lax.Precision.HIGHEST,
        preferred_element_type=jnp.float32,
    )


def kernel(x_any, flips_any, offs_any, out, sketch, gram, *scratch):
    (x, flips, offs, mixed, final, off_row, off_z, off_plane, off_pairs, off_all, packed, gram_xy,
     gram_core, gram_sum, gram_line, load_sems, sems, small_sems) = scratch[:18]
    held = [scratch[18 + 8 * i : 26 + 8 * i] for i in range(len(PARTS))]
    grp, dev = lax.axis_index("grp"), lax.axis_index("dev")
    zs, xy, line = (Team(grp, dev, kind) for kind in ("z", "xy", "line"))

    load_x = pltpu.make_async_copy(x_any, x, load_sems.at[0])
    load_f = pltpu.make_async_copy(flips_any, flips, load_sems.at[1])
    load_o = pltpu.make_async_copy(offs_any, offs, load_sems.at[2])
    barrier = pltpu.get_barrier_semaphore()
    for team in (xy, zs):
        if team is zs:
            load_f.start()
            load_x.start()
            load_o.start()
        team.each(
            lambda index, team=team: pl.semaphore_signal(
                barrier, inc=1, device_id=team.device(index), device_id_type=MESH
            )
        )

    def teams(i):
        return (zs, xy) if PARTS[i][2] else (xy, zs)

    def size(i):
        return PARTS[i][1] // SIDE

    def small(team, index, src, dst, phase):
        pltpu.make_async_remote_copy(
            src_ref=src,
            dst_ref=dst,
            send_sem=small_sems.at[0, phase],
            recv_sem=small_sems.at[1, phase],
            device_id=team.device(index),
            device_id_type=MESH,
        ).start()

    def small_done(block, side, phase):
        pltpu.make_async_copy(block, block, small_sems.at[side, phase]).wait()

    table = hadamard(LANES, SCALE)
    tables = jnp.concatenate([table, table], axis=1)
    load_f.wait()
    load_x.wait()
    for group in range(COLS // 8):
        values = []
        for blk in range(LOCAL // LANES):
            sign = (1 - 2 * flips[pl.ds(blk, 1), :]).astype(jnp.float32)
            values.append(x[pl.ds(group * 8, 8), pl.ds(blk * LANES, LANES)] * sign)
        for blk, value in enumerate(fwht(values)):
            mixed[pl.ds(blk * COLS + group * 8, 8), :] = value

    for i, (start, count, _) in enumerate(PARTS):
        for at in range(0, count, LANES):
            high, low = split(mixed[pl.ds(start + at, LANES), :])
            held[i][0][pl.ds(at, LANES), :] = lax.dot_general(
                tables,
                jnp.concatenate([high, low], axis=1),
                (((1,), (1,)), ((), ())),
                preferred_element_type=jnp.float32,
            )

    pl.semaphore_wait(barrier, zs.count + xy.count - 2)

    def scatter_outer(i):
        return teams(i)[0], held[i][0], held[i][1], 4 * i, size(i), False

    def scatter_inner(i):
        _, got, flat, turned, got_inner, _, _, _ = held[i]
        arrived(got, sems, 4 * i, size(i))
        mix(got, flat, size(i))
        to_inner(flat, turned, size(i))
        return teams(i)[1], turned, got_inner, 4 * i + 1, size(i), False

    def return_inner(i):
        got_inner, mid, back = held[i][4:7]
        arrived(got_inner, sems, 4 * i + 1, size(i))
        mix(got_inner, mid, size(i))
        return teams(i)[1], mid, back, 4 * i + 2, size(i), False

    def return_outer(i):
        back, flat = held[i][6:8]
        arrived(back, sems, 4 * i + 2, size(i))
        to_outer(back, flat, size(i))
        mine = final.at[pl.ds(PARTS[i][0], PARTS[i][1])]
        return teams(i)[0], flat, mine, 4 * i + 3, size(i), i == 1

    def finish(i):
        start, count, _ = PARTS[i]
        arrived(final.at[pl.ds(start, count)], sems, 4 * i + 3, size(i))
        for at in range(start, start + count, LANES):
            block = final[pl.ds(at, LANES), :].T
            for b in range(4):
                out[:, pl.ds((at // LANES * 4 + b) * LANES, LANES)] = block[b * COLS : (b + 1) * COLS]

    def product(i):
        return gram_of(held[i][5], PARTS[i], teams(i)[0].me, teams(i)[1].me, PARTS[i][2], off_all)

    exchange(sems, scatter_outer(0), scatter_outer(2))
    load_o.wait()
    lane = lax.broadcasted_iota(jnp.int32, (1, LANES), 1)
    row = jnp.zeros((1, LANES), jnp.int32)
    for k in range(SAMPLES):
        row = jnp.where(lane == k, offs[k], row)
    off_row[...] = row.astype(jnp.float32)[None]

    zs.each(lambda index: small(zs, index, off_row, off_z.at[pl.ds(zs.me, 1)], 0))
    off_z[pl.ds(zs.me, 1)] = off_row[...]
    exchange(sems, scatter_outer(1), scatter_outer(3))
    exchange(sems, scatter_inner(2))
    exchange(sems, scatter_inner(0))
    small_done(off_z.at[pl.ds(0, SIDE - 1)], 1, 0)
    for h in range(2):
        off_plane[0, pl.ds(h, 1), :] = tree_sum(
            pltpu.roll(off_z[8 * h + s], SAMPLES * s, 1) if s else off_z[8 * h] for s in range(8)
        )
    xy.each(lambda index: small(xy, index, off_plane, off_pairs.at[pl.ds(xy.me, 1)], 1))
    off_pairs[pl.ds(xy.me, 1)] = off_plane[...]
    exchange(sems, scatter_inner(3))
    exchange(sems, scatter_inner(1))
    exchange(sems, return_inner(2))
    exchange(sems, return_inner(0))
    exchange(sems, return_inner(3))
    exchange(sems, return_inner(1))
    small_done(off_pairs.at[pl.ds(0, SIDE - 1)], 1, 1)
    own = lax.broadcasted_iota(jnp.int32, (8, LANES), 1) // SAMPLES
    own = own == lax.broadcasted_iota(jnp.int32, (8, LANES), 0)
    for j in range(SIDE):
        for h in range(2):
            value = jnp.broadcast_to(off_pairs[j, pl.ds(h, 1), :], (8, LANES))
            off_all[pl.ds(j * SIDE + h * 8, 8), :] = jnp.where(own, value, -1.0)
    total = (product(0) + product(1)) + (product(2) + product(3))
    lane32 = lax.broadcasted_iota(jnp.int32, (COLS, LANES), 1) // COLS
    folded = tree_sum(
        jnp.where(lane32 == b, total[b * COLS : (b + 1) * COLS], 0.0) for b in range(4)
    )
    folded = folded + pltpu.roll(folded, 64, 1)
    folded = folded + pltpu.roll(folded, 32, 1)
    lane8 = lax.broadcasted_iota(jnp.int32, (8, LANES), 1) // COLS
    tile = tree_sum(
        jnp.where(lane8 == b, folded[b * 8 : (b + 1) * 8], 0.0) for b in range(4)
    )
    packed[...] = tile * (1.0 / TOTAL_SAMPLES)
    xy.each(lambda index: small(xy, index, packed, gram_xy.at[rows_at(xy.me, 8)], 2))
    gram_xy[rows_at(xy.me, 8), :] = packed[...]

    exchange(sems, return_outer(0))
    exchange(sems, return_outer(2))
    small_done(gram_xy.at[pl.ds(0, 8 * (xy.count - 1))], 1, 2)
    gram_core[pl.ds(0, 8), :] = tree_sum(gram_xy[pl.ds(8 * j, 8), :] for j in range(xy.count))
    small(zs, zs.me + 1 - 2 * zs.core, gram_core.at[pl.ds(0, 8)], gram_core.at[pl.ds(8, 8)], 3)

    exchange(sems, return_outer(1))
    exchange(sems, return_outer(3))
    small_done(gram_core.at[pl.ds(8, 8)], 1, 3)
    gram_sum[...] = gram_core[pl.ds(0, 8), :] + gram_core[pl.ds(8, 8), :]
    line.each(lambda index: small(line, index, gram_sum, gram_line.at[rows_at(line.me, 8)], 4))
    gram_line[rows_at(line.me, 8), :] = gram_sum[...]

    finish(2)
    finish(0)
    finish(3)
    for i in range(len(PARTS)):
        for phase in range(3):
            sent(held[i][1], sems, 4 * i + phase, size(i))
    small_done(gram_line.at[pl.ds(0, 8 * (line.count - 1))], 1, 4)
    whole = tree_sum(gram_line[pl.ds(8 * j, 8), :] for j in range(line.count))
    for b in range(4):
        turned = pltpu.roll(whole, LANES - COLS * b, 1) if b else whole
        gram[pl.ds(b * 8, 8), :] = turned[:, :COLS]
    finish(1)

    picked = []
    for k in range(SAMPLES):
        at = offs[k]
        value = final[pl.ds((at // 512) * LANES + at % LANES, 1), :]
        picked.append(jnp.where(lane // COLS == (at // LANES) % 4, value, 0.0))
    picked = jnp.concatenate(picked, axis=0)
    picked = picked + pltpu.roll(picked, 64, 1)
    picked = picked + pltpu.roll(picked, 32, 1)
    sketch[...] = picked[:, :COLS]

    for i in range(len(PARTS)):
        sent(held[i][1], sems, 4 * i + 3, size(i))
    small_done(off_z.at[pl.ds(0, SIDE - 1)], 0, 0)
    small_done(off_pairs.at[pl.ds(0, SIDE - 1)], 0, 1)
    small_done(gram_xy.at[pl.ds(0, 8 * (xy.count - 1))], 0, 2)
    small_done(gram_core.at[pl.ds(8, 8)], 0, 3)
    small_done(gram_line.at[pl.ds(0, 8 * (line.count - 1))], 0, 4)


def store(*refs):
    sems = refs[6]
    copies = []
    for i in range(3):
        copies.append(pltpu.make_async_copy(refs[i], refs[3 + i], sems.at[i]))
        copies[-1].start()
    for copy in copies:
        copy.wait()


def local(matrix_slab, sign_flips, sample_offset):
    f32 = jnp.float32
    scratch = [
        pltpu.VMEM((COLS, LOCAL), f32),
        pltpu.VMEM((LOCAL // LANES, LANES), jnp.int32),
        pltpu.SMEM((SAMPLES,), jnp.int32),
        pltpu.VMEM((ROWS, LANES), f32),
        pltpu.VMEM((ROWS, LANES), f32),
        pltpu.VMEM((1, 1, LANES), f32),
        pltpu.VMEM((SIDE, 1, LANES), f32),
        pltpu.VMEM((1, 2, LANES), f32),
        pltpu.VMEM((SIDE, 2, LANES), f32),
        pltpu.VMEM((SIDE * SIDE, LANES), f32),
        pltpu.VMEM((8, LANES), f32),
        pltpu.VMEM((SIDE * 8, LANES), f32),
        pltpu.VMEM((2 * 8, LANES), f32),
        pltpu.VMEM((8, LANES), f32),
        pltpu.VMEM((8 * 8, LANES), f32),
        pltpu.SemaphoreType.DMA((3,)),
        pltpu.SemaphoreType.DMA((2, 4 * len(PARTS))),
        pltpu.SemaphoreType.DMA((2, 5)),
    ]
    for _, count, _ in PARTS:
        scratch += [pltpu.VMEM((count, LANES), f32)] * 8
    shapes = (
        jax.ShapeDtypeStruct((COLS, LOCAL), f32),
        jax.ShapeDtypeStruct((SAMPLES, COLS), f32),
        jax.ShapeDtypeStruct((COLS, COLS), f32),
    )
    args = (matrix_slab, sign_flips.reshape(LOCAL // LANES, LANES), sample_offset)
    args = [pltpu.with_memory_space_constraint(arg, pltpu.HBM) for arg in args]
    results = pl.pallas_call(
        kernel,
        out_shape=shapes,
        in_specs=[pl.BlockSpec(memory_space=pl.ANY)] * 3,
        out_specs=[pl.BlockSpec(memory_space=pltpu.VMEM)] * 3,
        scratch_shapes=scratch,
        compiler_params=pltpu.CompilerParams(
            collective_id=0, has_side_effects=True, vmem_limit_bytes=24 << 20
        ),
        name="hadamard",
    )(*args)
    transformed, sketch, gram = pl.pallas_call(
        store,
        out_shape=shapes,
        in_specs=[pl.BlockSpec(memory_space=pl.ANY)] * 3,
        out_specs=[pl.BlockSpec(memory_space=pl.ANY)] * 3,
        scratch_shapes=[pltpu.SemaphoreType.DMA((3,))],
        compiler_params=pltpu.CompilerParams(vmem_limit_bytes=1 << 20),
        name="store",
    )(*(pltpu.with_memory_space_constraint(value, pltpu.VMEM) for value in results))
    return transformed, sketch.T, gram


def solution(mesh):
    return jax.shard_map(
        local,
        mesh=mesh,
        in_specs=(P(None, ("grp", "dev")), P(("grp", "dev")), P(("grp", "dev"))),
        out_specs=(P(None, ("grp", "dev")), P(None, ("grp", "dev")), P()),
        check_vma=False,
    )
```

```python
import functools

import jax
import jax.numpy as jnp
from jax import lax
from jax.experimental import pallas as pl
from jax.experimental.pallas import tpu as pltpu
from jax.sharding import PartitionSpec as P

MESH = pl.DeviceIdType.MESH
LANES = 128
SIDE = 16
COLS = 32
LOCAL = 4096
SAMPLES = 16
TOTAL_SAMPLES = 4096
ROWS = LOCAL * COLS // LANES
SCALE = 2.0**-10
PARTS = ((0, 256, True), (256, 256, True), (512, 256, False), (768, 256, False))


def fwht(values):
    values = list(values)
    step = 1
    while step < len(values):
        for low in range(0, len(values), 2 * step):
            for at in range(low, low + step):
                a, b = values[at], values[at + step]
                values[at], values[at + step] = a + b, a - b
        step *= 2
    return values


def tree_sum(values):
    values = list(values)
    while len(values) > 1:
        values = [values[i] + values[i + 1] for i in range(0, len(values), 2)]
    return values[0]


def split(value):
    high = value.astype(jnp.bfloat16)
    low = (value - high.astype(jnp.float32)).astype(jnp.bfloat16)
    return high, low


def hadamard(order, scale):
    shape = (order, order)
    common = lax.broadcasted_iota(jnp.int32, shape, 0) & lax.broadcasted_iota(jnp.int32, shape, 1)
    bits = order.bit_length() - 1
    parity = common & 1
    for position in range(1, bits):
        parity = parity ^ ((common >> position) & 1)
    return jnp.where(parity == 1, -scale, scale).astype(jnp.bfloat16)


def wrap(value, count):
    return jnp.where(value >= count, value - count, value)


class Team:
    def __init__(self, grp, dev, kind):
        self.kind = kind
        self.high, self.low = lax.div(dev, 16), lax.rem(dev, 16)
        self.grp, self.core = grp, lax.rem(grp, 2)
        self.me, self.count = {
            "z": (8 * self.high + grp, 16),
            "xy": (self.low, 16),
            "line": (4 * self.high + lax.div(grp, 2), 8),
        }[kind]

    def device(self, index):
        if self.kind == "z":
            upper = index >= 8
            return (jnp.where(upper, index - 8, index), jnp.where(upper, self.low + 16, self.low))
        if self.kind == "xy":
            return (self.grp, self.high * 16 + index)
        upper = index >= 4
        near = jnp.where(upper, index - 4, index)
        return (near * 2 + self.core, jnp.where(upper, self.low + 16, self.low))

    def partner(self, turn):
        away = lax.div(turn + 1, 2)
        apart = self.count // 2 + away * (1 - 2 * lax.rem(turn, 2))
        return wrap(self.me + apart, self.count)

    def ranked(self, turn):
        index = jnp.where(turn < 8, turn + 1 - 2 * lax.rem(turn, 2), 23 - turn)
        return jnp.where(self.me == index, 8, index)

    def each(self, body):
        def step(turn, carry):
            body(self.partner(turn))
            return carry

        lax.fori_loop(0, self.count - 1, step, 0, unroll=True)


def rows_at(index, count):
    return pl.ds(pl.multiple_of(index * count, 8), count)


def exchange(sems, *jobs):
    def step(turn, carry):
        for team, src, dst, phase, size, ranked in jobs:
            index = team.ranked(turn) if ranked else team.partner(turn)
            pltpu.make_async_remote_copy(
                src_ref=src.at[rows_at(index, size)],
                dst_ref=dst.at[rows_at(team.me, size)],
                send_sem=sems.at[0, phase],
                recv_sem=sems.at[1, phase],
                device_id=team.device(index),
                device_id_type=MESH,
            ).start()
        return carry

    lax.fori_loop(0, SIDE - 1, step, 0, unroll=True)
    for team, src, dst, phase, size, _ in jobs:
        mine = rows_at(team.me, size)
        dst[mine, :] = src[mine, :]


def arrived(dst, sems, phase, size):
    block = dst.at[pl.ds(0, (SIDE - 1) * size)]
    pltpu.make_async_copy(block, block, sems.at[1, phase]).wait()


def sent(dst, sems, phase, size):
    block = dst.at[pl.ds(0, (SIDE - 1) * size)]
    pltpu.make_async_copy(block, block, sems.at[0, phase]).wait()


def mix(src, dst, size):
    def tile(at, carry):
        values = [src[pl.ds(pl.multiple_of(j * size + at * 8, 8), 8), :] for j in range(SIDE)]
        for j, value in enumerate(fwht(values)):
            dst[pl.ds(pl.multiple_of(j * size + at * 8, 8), 8), :] = value
        return carry

    lax.fori_loop(0, size // 8, tile, 0)


def to_inner(src, dst, size):
    def block(at, carry):
        for half in range(2):
            rows = src[pl.ds(at + half * 8 * size, 8, stride=size), :]
            dst[pl.ds(pl.multiple_of(at * SIDE + half * 8, 8), 8), :] = rows
        return carry

    lax.fori_loop(0, size, block, 0, unroll=8)


def to_outer(src, dst, size):
    def block(at, carry):
        for tile in range(size // 8):
            rows = src[pl.ds(at + tile * 8 * SIDE, 8, stride=SIDE), :]
            dst[pl.ds(pl.multiple_of(at * size + tile * 8, 8), 8), :] = rows
        return carry

    lax.fori_loop(0, SIDE, block, 0, unroll=4)


def gram_of(mid, part, first, outer, inner_along_z, offsets):
    start, count, _ = part
    size = count // SIDE
    marks = [[] for _ in range(4)]
    for j in range(SIDE):
        for r in range(size // 16):
            row = start + first * size + outer * (size // 16) + r
            place = lax.div(row, LANES) * 4 * LANES + lax.rem(row, LANES)
            for half in range(2):
                if inner_along_z:
                    held = offsets[pl.ds(j * SIDE + half * 8, 8), :]
                else:
                    held = offsets[pl.ds(j + half * 8 * SIDE, 8, stride=SIDE), :]
                for b in range(4):
                    here = held == (place + b * LANES).astype(jnp.float32)
                    marks[b].append(jnp.where(here, 1.0, 0.0))
    marks = jnp.concatenate([jnp.concatenate(m, axis=0) for m in marks], axis=1)
    a = lax.broadcasted_iota(jnp.int32, (4 * LANES, LANES), 0) // LANES
    b = lax.broadcasted_iota(jnp.int32, (4 * LANES, LANES), 1) // COLS
    spread = jnp.where(a == b, 1.0, 0.0).astype(jnp.bfloat16)
    counts = jnp.dot(marks.astype(jnp.bfloat16), spread, preferred_element_type=jnp.float32)
    values = mid[...]
    return lax.dot_general(
        values,
        counts * values,
        (((0,), (0,)), ((), ())),
        precision=lax.Precision.HIGHEST,
        preferred_element_type=jnp.float32,
    )


def kernel(x_any, flips_any, offs_any, out, sketch, gram, *scratch):
    (x, flips, offs, mixed, final, off_row, off_z, off_plane, off_pairs, off_all, packed, gram_xy,
     gram_core, gram_sum, gram_line, load_sems, sems, small_sems) = scratch[:18]
    held = [scratch[18 + 8 * i : 26 + 8 * i] for i in range(len(PARTS))]
    grp, dev = lax.axis_index("grp"), lax.axis_index("dev")
    zs, xy, line = (Team(grp, dev, kind) for kind in ("z", "xy", "line"))

    load_x = pltpu.make_async_copy(x_any, x, load_sems.at[0])
    load_f = pltpu.make_async_copy(flips_any, flips, load_sems.at[1])
    load_o = pltpu.make_async_copy(offs_any, offs, load_sems.at[2])
    barrier = pltpu.get_barrier_semaphore()
    for team in (xy, zs):
        if team is zs:
            load_f.start()
            load_x.start()
            load_o.start()
        team.each(
            lambda index, team=team: pl.semaphore_signal(
                barrier, inc=1, device_id=team.device(index), device_id_type=MESH
            )
        )

    def teams(i):
        return (zs, xy) if PARTS[i][2] else (xy, zs)

    def size(i):
        return PARTS[i][1] // SIDE

    def small(team, index, src, dst, phase):
        pltpu.make_async_remote_copy(
            src_ref=src,
            dst_ref=dst,
            send_sem=small_sems.at[0, phase],
            recv_sem=small_sems.at[1, phase],
            device_id=team.device(index),
            device_id_type=MESH,
        ).start()

    def small_done(block, side, phase):
        pltpu.make_async_copy(block, block, small_sems.at[side, phase]).wait()

    table = hadamard(LANES, SCALE)
    tables = jnp.concatenate([table, table], axis=1)
    load_f.wait()
    load_x.wait()
    for group in range(COLS // 8):
        values = []
        for blk in range(LOCAL // LANES):
            sign = (1 - 2 * flips[pl.ds(blk, 1), :]).astype(jnp.float32)
            values.append(x[pl.ds(group * 8, 8), pl.ds(blk * LANES, LANES)] * sign)
        for blk, value in enumerate(fwht(values)):
            mixed[pl.ds(blk * COLS + group * 8, 8), :] = value

    for i, (start, count, _) in enumerate(PARTS):
        for at in range(0, count, LANES):
            high, low = split(mixed[pl.ds(start + at, LANES), :])
            held[i][0][pl.ds(at, LANES), :] = lax.dot_general(
                tables,
                jnp.concatenate([high, low], axis=1),
                (((1,), (1,)), ((), ())),
                preferred_element_type=jnp.float32,
            )

    pl.semaphore_wait(barrier, zs.count + xy.count - 2)

    def scatter_outer(i):
        return teams(i)[0], held[i][0], held[i][1], 4 * i, size(i), False

    def scatter_inner(i):
        _, got, flat, turned, got_inner, _, _, _ = held[i]
        arrived(got, sems, 4 * i, size(i))
        mix(got, flat, size(i))
        to_inner(flat, turned, size(i))
        return teams(i)[1], turned, got_inner, 4 * i + 1, size(i), False

    def return_inner(i):
        got_inner, mid, back = held[i][4:7]
        arrived(got_inner, sems, 4 * i + 1, size(i))
        mix(got_inner, mid, size(i))
        return teams(i)[1], mid, back, 4 * i + 2, size(i), False

    def return_outer(i):
        back, flat = held[i][6:8]
        arrived(back, sems, 4 * i + 2, size(i))
        to_outer(back, flat, size(i))
        mine = final.at[pl.ds(PARTS[i][0], PARTS[i][1])]
        return teams(i)[0], flat, mine, 4 * i + 3, size(i), i == 1

    def finish(i):
        start, count, _ = PARTS[i]
        arrived(final.at[pl.ds(start, count)], sems, 4 * i + 3, size(i))
        for at in range(start, start + count, LANES):
            block = final[pl.ds(at, LANES), :].T
            for b in range(4):
                out[:, pl.ds((at // LANES * 4 + b) * LANES, LANES)] = block[b * COLS : (b + 1) * COLS]

    def product(i):
        return gram_of(held[i][5], PARTS[i], teams(i)[0].me, teams(i)[1].me, PARTS[i][2], off_all)

    exchange(sems, scatter_outer(0), scatter_outer(2))
    load_o.wait()
    lane = lax.broadcasted_iota(jnp.int32, (1, LANES), 1)
    row = jnp.zeros((1, LANES), jnp.int32)
    for k in range(SAMPLES):
        row = jnp.where(lane == k, offs[k], row)
    off_row[...] = row.astype(jnp.float32)[None]

    zs.each(lambda index: small(zs, index, off_row, off_z.at[pl.ds(zs.me, 1)], 0))
    off_z[pl.ds(zs.me, 1)] = off_row[...]
    exchange(sems, scatter_outer(1), scatter_outer(3))
    exchange(sems, scatter_inner(2))
    exchange(sems, scatter_inner(0))
    small_done(off_z.at[pl.ds(0, SIDE - 1)], 1, 0)
    for h in range(2):
        off_plane[0, pl.ds(h, 1), :] = tree_sum(
            pltpu.roll(off_z[8 * h + s], SAMPLES * s, 1) if s else off_z[8 * h] for s in range(8)
        )
    xy.each(lambda index: small(xy, index, off_plane, off_pairs.at[pl.ds(xy.me, 1)], 1))
    off_pairs[pl.ds(xy.me, 1)] = off_plane[...]
    exchange(sems, scatter_inner(3))
    exchange(sems, scatter_inner(1))
    exchange(sems, return_inner(2))
    exchange(sems, return_inner(0))
    exchange(sems, return_inner(3))
    exchange(sems, return_inner(1))
    small_done(off_pairs.at[pl.ds(0, SIDE - 1)], 1, 1)
    own = lax.broadcasted_iota(jnp.int32, (8, LANES), 1) // SAMPLES
    own = own == lax.broadcasted_iota(jnp.int32, (8, LANES), 0)
    for j in range(SIDE):
        for h in range(2):
            value = jnp.broadcast_to(off_pairs[j, pl.ds(h, 1), :], (8, LANES))
            off_all[pl.ds(j * SIDE + h * 8, 8), :] = jnp.where(own, value, -1.0)
    total = (product(0) + product(1)) + (product(2) + product(3))
    lane32 = lax.broadcasted_iota(jnp.int32, (COLS, LANES), 1) // COLS
    folded = tree_sum(
        jnp.where(lane32 == b, total[b * COLS : (b + 1) * COLS], 0.0) for b in range(4)
    )
    folded = folded + pltpu.roll(folded, 64, 1)
    folded = folded + pltpu.roll(folded, 32, 1)
    lane8 = lax.broadcasted_iota(jnp.int32, (8, LANES), 1) // COLS
    tile = tree_sum(
        jnp.where(lane8 == b, folded[b * 8 : (b + 1) * 8], 0.0) for b in range(4)
    )
    packed[...] = tile * (1.0 / TOTAL_SAMPLES)
    xy.each(lambda index: small(xy, index, packed, gram_xy.at[rows_at(xy.me, 8)], 2))
    gram_xy[rows_at(xy.me, 8), :] = packed[...]

    exchange(sems, return_outer(0))
    exchange(sems, return_outer(2))
    exchange(sems, return_outer(1))
    small_done(gram_xy.at[pl.ds(0, 8 * (xy.count - 1))], 1, 2)
    gram_core[pl.ds(0, 8), :] = tree_sum(gram_xy[pl.ds(8 * j, 8), :] for j in range(xy.count))
    small(zs, zs.me + 1 - 2 * zs.core, gram_core.at[pl.ds(0, 8)], gram_core.at[pl.ds(8, 8)], 3)

    exchange(sems, return_outer(3))
    small_done(gram_core.at[pl.ds(8, 8)], 1, 3)
    gram_sum[...] = gram_core[pl.ds(0, 8), :] + gram_core[pl.ds(8, 8), :]
    line.each(lambda index: small(line, index, gram_sum, gram_line.at[rows_at(line.me, 8)], 4))
    gram_line[rows_at(line.me, 8), :] = gram_sum[...]

    finish(2)
    finish(0)
    finish(3)
    for i in range(len(PARTS)):
        for phase in range(3):
            sent(held[i][1], sems, 4 * i + phase, size(i))
    small_done(gram_line.at[pl.ds(0, 8 * (line.count - 1))], 1, 4)
    whole = tree_sum(gram_line[pl.ds(8 * j, 8), :] for j in range(line.count))
    for b in range(4):
        turned = pltpu.roll(whole, LANES - COLS * b, 1) if b else whole
        gram[pl.ds(b * 8, 8), :] = turned[:, :COLS]
    finish(1)

    picked = []
    for k in range(SAMPLES):
        at = offs[k]
        value = final[pl.ds((at // 512) * LANES + at % LANES, 1), :]
        picked.append(jnp.where(lane // COLS == (at // LANES) % 4, value, 0.0))
    picked = jnp.concatenate(picked, axis=0)
    picked = picked + pltpu.roll(picked, 64, 1)
    picked = picked + pltpu.roll(picked, 32, 1)
    sketch[...] = picked[:, :COLS]

    for i in range(len(PARTS)):
        sent(held[i][1], sems, 4 * i + 3, size(i))
    small_done(off_z.at[pl.ds(0, SIDE - 1)], 0, 0)
    small_done(off_pairs.at[pl.ds(0, SIDE - 1)], 0, 1)
    small_done(gram_xy.at[pl.ds(0, 8 * (xy.count - 1))], 0, 2)
    small_done(gram_core.at[pl.ds(8, 8)], 0, 3)
    small_done(gram_line.at[pl.ds(0, 8 * (line.count - 1))], 0, 4)


def store(*refs):
    sems = refs[6]
    copies = []
    for i in range(3):
        copies.append(pltpu.make_async_copy(refs[i], refs[3 + i], sems.at[i]))
        copies[-1].start()
    for copy in copies:
        copy.wait()


def local(matrix_slab, sign_flips, sample_offset):
    f32 = jnp.float32
    scratch = [
        pltpu.VMEM((COLS, LOCAL), f32),
        pltpu.VMEM((LOCAL // LANES, LANES), jnp.int32),
        pltpu.SMEM((SAMPLES,), jnp.int32),
        pltpu.VMEM((ROWS, LANES), f32),
        pltpu.VMEM((ROWS, LANES), f32),
        pltpu.VMEM((1, 1, LANES), f32),
        pltpu.VMEM((SIDE, 1, LANES), f32),
        pltpu.VMEM((1, 2, LANES), f32),
        pltpu.VMEM((SIDE, 2, LANES), f32),
        pltpu.VMEM((SIDE * SIDE, LANES), f32),
        pltpu.VMEM((8, LANES), f32),
        pltpu.VMEM((SIDE * 8, LANES), f32),
        pltpu.VMEM((2 * 8, LANES), f32),
        pltpu.VMEM((8, LANES), f32),
        pltpu.VMEM((8 * 8, LANES), f32),
        pltpu.SemaphoreType.DMA((3,)),
        pltpu.SemaphoreType.DMA((2, 4 * len(PARTS))),
        pltpu.SemaphoreType.DMA((2, 5)),
    ]
    for _, count, _ in PARTS:
        scratch += [pltpu.VMEM((count, LANES), f32)] * 8
    shapes = (
        jax.ShapeDtypeStruct((COLS, LOCAL), f32),
        jax.ShapeDtypeStruct((SAMPLES, COLS), f32),
        jax.ShapeDtypeStruct((COLS, COLS), f32),
    )
    args = (matrix_slab, sign_flips.reshape(LOCAL // LANES, LANES), sample_offset)
    args = [pltpu.with_memory_space_constraint(arg, pltpu.HBM) for arg in args]
    results = pl.pallas_call(
        kernel,
        out_shape=shapes,
        in_specs=[pl.BlockSpec(memory_space=pl.ANY)] * 3,
        out_specs=[pl.BlockSpec(memory_space=pltpu.VMEM)] * 3,
        scratch_shapes=scratch,
        compiler_params=pltpu.CompilerParams(
            collective_id=0, has_side_effects=True, vmem_limit_bytes=24 << 20
        ),
        name="hadamard",
    )(*args)
    transformed, sketch, gram = pl.pallas_call(
        store,
        out_shape=shapes,
        in_specs=[pl.BlockSpec(memory_space=pl.ANY)] * 3,
        out_specs=[pl.BlockSpec(memory_space=pl.ANY)] * 3,
        scratch_shapes=[pltpu.SemaphoreType.DMA((3,))],
        compiler_params=pltpu.CompilerParams(vmem_limit_bytes=1 << 20),
        name="store",
    )(*(pltpu.with_memory_space_constraint(value, pltpu.VMEM) for value in results))
    return transformed, sketch.T, gram


def solution(mesh):
    return jax.shard_map(
        local,
        mesh=mesh,
        in_specs=(P(None, ("grp", "dev")), P(("grp", "dev")), P(("grp", "dev"))),
        out_specs=(P(None, ("grp", "dev")), P(None, ("grp", "dev")), P()),
        check_vma=False,
    )
```
